32 devices in a mesh: img: 16 (over z, x, core), scale: 2 (over y).
Axes of the slice: x: 2, y: 2, z: 4, core: 2. Of those that a mesh axis runs over, the one named last changes fastest.
Arguments:
- features: bfloat16 [16, 2, 24, 24, 256], P('img', 'scale'), may hold values from -6 to 6
- extents: int32 [16, 2], P('img'), may hold values from 12 to 24, as said below
- canvas_large: int32 [16], P('img'), may hold values from 0 to 1
- label_mask: int32 [16, 24, 24], P('img', 'scale'), may hold values 0 or 1
- kernel_one: bfloat16 [2304, 512], replicated, may hold values from -0.125 to 0.125
- kernel_two: bfloat16 [4608, 512], replicated, may hold values from -0.09375 to 0.09375
- kernel_three: bfloat16 [4608, 512], replicated, may hold values from -0.09375 to 0.09375
- kernel_four: bfloat16 [4608, 512], replicated, may hold values from -0.09375 to 0.09375
- kernel_five: bfloat16 [4608, 512], replicated, may hold values from -0.09375 to 0.09375
- kernel_six: bfloat16 [4608, 512], replicated, may hold values from -0.09375 to 0.09375
- affine_scale: float32 [6, 512], replicated, may hold values from 1 to 2.5
- affine_shift: float32 [6, 512], replicated, may hold values from -0.5 to 0.5
- head_lower: bfloat16 [512, 1792], replicated, may hold values from -0.25 to 0.25
- head_upper: bfloat16 [512, 1792], replicated, may hold values from -0.25 to 0.25
- gain_lower: float32 [1792], replicated, may hold values from 4 to 32
- gain_upper: float32 [1792], replicated, may hold values from 4 to 32
- merged_grad: bfloat16 [16, 24, 24, 1792], P('img', 'scale'), may hold values from -6 to 6
Outputs:
- merged: bfloat16 [16, 24, 24, 1792], P('img', 'scale')
- features_grad: bfloat16 [16, 2, 24, 24, 256], P('img', 'scale')
- kernel_one_grad: float32 [1179648], P(('img', 'scale'))
- kernel_two_grad: float32 [2359296], P(('img', 'scale'))
- kernel_three_grad: float32 [2359296], P(('img', 'scale'))
- kernel_four_grad: float32 [2359296], P(('img', 'scale'))
- kernel_five_grad: float32 [2359296], P(('img', 'scale'))
- kernel_six_grad: float32 [2359296], P(('img', 'scale'))
- head_lower_grad: float32 [917504], P(('img', 'scale'))
- head_upper_grad: float32 [917504], P(('img', 'scale'))
- gain_lower_grad: float32 [1792], P(('img', 'scale'))
- gain_upper_grad: float32 [1792], P(('img', 'scale'))
The draws below stay inside these ranges and needn't reach their ends.
Inputs may be any that keep to these rules, and one draw needn't show every extreme that they name: `extents`: each row is an image's height and width at the finest scale; some image has both equal to 24 and another both equal to 12. `canvas_large`: the index along scale of the canvas with the finest scale; the other canvas holds the two coarser ones.
All inputs are finite; a program needn't handle non-finite values. No bound on the sum of `label_mask` on one device may be relied on, other than what follows from the above.
Results may differ from the reference program's by a relative error of at most 0.025.
Values may be sent and summed in bfloat16 or wider, within the bound.
No kernel may reach another device: no remote copies, remote signals or barrier semaphores. Data moves between devices by JAX's collectives and lax.ppermute only.
A program may use at most 256 MiB of HBM per device.

```python
import math
import jax
import jax.numpy as jnp
from jax import lax

C_IN = 256
C_MID = 512
TASKS = 7
TASK_C = 256
HEAD_OUT = 1792
CANVAS = 24
IMAGES = 16
N_SCALE = 2


def draw_extents(key, part):
    key = jax.random.fold_in(key, 11)
    subkeys = jax.random.split(key, 3)
    extent_values = jax.random.randint(subkeys[0], (IMAGES, 2), CANVAS // 2, CANVAS + 1)
    widest = jax.random.randint(subkeys[1], (), 0, IMAGES)
    narrowest = (widest + 1 + jax.random.randint(subkeys[2], (), 0, IMAGES - 1)) % IMAGES
    extent_values = extent_values.at[narrowest].set(CANVAS // 2)
    extent_values = extent_values.at[widest].set(CANVAS)
    return extent_values.astype(jnp.int32)


def set_ends(result, rng, least, largest):
    longest = result.shape.index(max(result.shape))
    spots = []
    for shift in (0, 1):
        where = [jax.random.randint(jax.random.fold_in(rng, axis), (), 0, length) for axis, length in enumerate(result.shape)]
        where[longest] = (where[longest] + shift) % result.shape[longest]
        spots.append(tuple(where))
    return result.at[spots[0]].set(least).at[spots[1]].set(largest)


def steps_of(stream_key, shape, shards, least, largest):
    level = 1.0
    for dim, blocks in shards:
        heights = jax.random.uniform(jax.random.fold_in(jax.random.fold_in(stream_key, 6), dim), (blocks,), jnp.float32, least / len(shards), largest / len(shards))
        level = level * jnp.repeat(jnp.exp(heights), shape[dim] // blocks).reshape((-1,) + (1,) * (len(shape) - 1 - dim))
    return level


def noise(key, shape, scale, reach, cuts=(), held_as=jnp.bfloat16):
    values = jax.random.normal(key, shape, jnp.float32) * scale
    if len(cuts) > 0:
        values = steps_of(key, shape, cuts, -0.22, 0.18) * values
    return jnp.clip(values, min=-reach, max=reach).astype(held_as)


def setup_inputs(seed: int = 0) -> dict:
    streams_of = jax.random.split(jax.random.key(seed), 18)
    return {
        "features": noise(streams_of[0], (IMAGES, N_SCALE, CANVAS, CANVAS, C_IN), 1.0, 6.0, ((0, 16), (1, 2))),
        "extents": draw_extents(jax.random.fold_in(streams_of[17], 71), 0),
        "canvas_large": set_ends(jax.random.randint(streams_of[2], (IMAGES,), 0, 2), jax.random.fold_in(streams_of[2], 1), 0, 1).astype(jnp.int32),
        "label_mask": set_ends((jax.random.randint(streams_of[3], (IMAGES, CANVAS, CANVAS), 0, 4) < 3).astype(jnp.int32), jax.random.fold_in(streams_of[3], 1), 0, 1),
        "kernel_one": noise(streams_of[4], (9 * C_IN, C_MID), (9 * C_IN) ** -0.5, 0.125),
        "kernel_two": noise(streams_of[5], (9 * C_MID, C_MID), (9 * C_MID) ** -0.5, 0.09375),
        "kernel_three": noise(streams_of[6], (9 * C_MID, C_MID), (9 * C_MID) ** -0.5, 0.09375),
        "kernel_four": noise(streams_of[7], (9 * C_MID, C_MID), (9 * C_MID) ** -0.5, 0.09375),
        "kernel_five": noise(streams_of[8], (9 * C_MID, C_MID), (9 * C_MID) ** -0.5, 0.09375),
        "kernel_six": noise(streams_of[9], (9 * C_MID, C_MID), (9 * C_MID) ** -0.5, 0.09375),
        "affine_scale": jnp.clip(jnp.exp(jax.random.uniform(streams_of[10], (6, C_MID), jnp.float32, math.log(1.0), math.log(2.5))), 1.0, 2.5),
        "affine_shift": jnp.clip(jax.random.uniform(streams_of[11], (6, C_MID), jnp.float32, -0.5, 0.5), -0.5, 0.5),
        "head_lower": noise(streams_of[12], (C_MID, HEAD_OUT), C_MID ** -0.5, 0.25),
        "head_upper": noise(streams_of[13], (C_MID, HEAD_OUT), C_MID ** -0.5, 0.25),
        "gain_lower": jnp.clip(jnp.exp(jax.random.uniform(streams_of[14], (HEAD_OUT,), jnp.float32, math.log(4.0), math.log(32.0))), 4.0, 32.0),
        "gain_upper": jnp.clip(jnp.exp(jax.random.uniform(streams_of[15], (HEAD_OUT,), jnp.float32, math.log(4.0), math.log(32.0))), 4.0, 32.0),
        "merged_grad": noise(streams_of[16], (IMAGES, CANVAS, CANVAS, HEAD_OUT), 1.0, 6.0, ((0, 16), (1, 2))),
    }


@jax.custom_vjp
def low(v):
    return lax.optimization_barrier(v.astype(jnp.bfloat16)).astype(jnp.float32)

@jax.custom_vjp
def low_back(v):
    return v

def low_keep(v):
    return (low(v), None)

def low_pass(kept, grad):
    return (grad,)

def back_keep(v):
    return (v, None)

def back_low(kept, grad):
    return (low(grad),)
low.defvjp(low_keep, low_pass)
low_back.defvjp(back_keep, back_low)

def geometry(extent):
    height = extent[0]
    breadth = extent[1]
    start_col = CANVAS // 2 + 2
    places = jnp.arange(CANVAS, dtype=jnp.int32)
    row_index = places[:, None]
    col_index = places[None, :]
    large_mask = (row_index < height) & (col_index < breadth)
    small_mask = (row_index < height // 2) & (col_index < breadth // 2) | (row_index < height // 4) & (col_index >= start_col) & (col_index < start_col + breadth // 4)
    row_source = jnp.stack([places, places * (height // 2) // height, places * (height // 4) // height])
    col_source = jnp.stack([places, places * (breadth // 2) // breadth, start_col + places * (breadth // 4) // breadth])
    row_valid = (places < height)[None, :, None]
    col_valid = (places < breadth)[None, :, None]
    row_ops = ((row_source[:, :, None] == places[None, None, :]) & row_valid).astype(jnp.float32)
    col_ops = ((col_source[:, :, None] == places[None, None, :]) & col_valid).astype(jnp.float32)
    return (large_mask, small_mask, row_ops, col_ops)

def unfold(fields, dilation):
    padded = jnp.pad(fields, ((0, 0), (dilation, dilation), (dilation, dilation), (0, 0)))
    pieces = [padded[:, row_tap * dilation:row_tap * dilation + CANVAS, col_tap * dilation:col_tap * dilation + CANVAS, :] for row_tap in range(3) for col_tap in range(3)]
    return jnp.concatenate(pieces, axis=-1)

def image_forward(kernels, heads, gains, affine_scale, affine_shift, image, extent, biggest):
    large_mask, small_mask, row_ops, col_ops = geometry(extent)
    chosen = (jnp.arange(N_SCALE, dtype=jnp.int32) == biggest)[:, None, None]
    masks = jnp.where(chosen, large_mask[None], small_mask[None]).astype(jnp.float32)[..., None]
    current = image * masks
    tapped = []
    for depth in range(6):
        dilation = 1 if depth < 3 else 2
        entered = low(current)
        if depth == 3:
            tapped.append(entered)
        columns = unfold(entered, dilation)
        linear = jnp.dot(columns.reshape(-1, columns.shape[-1]), kernels[depth], precision=lax.Precision.HIGHEST)
        linear = low_back(linear.reshape(N_SCALE, CANVAS, CANVAS, C_MID))
        current = masks * jax.nn.gelu(affine_scale[depth] * linear + affine_shift[depth])
    tapped.append(low(current))
    tap_total = jnp.zeros((N_SCALE, CANVAS, CANVAS, HEAD_OUT), jnp.float32)
    for branch in range(2):
        project = jnp.dot(tapped[branch].reshape(-1, C_MID), heads[branch], precision=lax.Precision.HIGHEST)
        project = low_back(project).reshape(-1, TASKS, TASK_C)
        normed = project * lax.rsqrt(lax.optimization_barrier(jnp.sum(project * project, axis=-1, keepdims=True)) + 1e-06)
        tap_total = tap_total + low(normed.reshape(N_SCALE, CANVAS, CANVAS, HEAD_OUT) * gains[branch])
    merged = jnp.zeros((CANVAS, CANVAS, HEAD_OUT), jnp.float32)
    for level in range(3):
        source = biggest if level == 0 else 1 - biggest
        canvas = lax.dynamic_index_in_dim(tap_total, source, 0, keepdims=False)
        stretched = jnp.einsum('ya,abc->ybc', row_ops[level], canvas, precision=lax.Precision.HIGHEST)
        merged = merged + jnp.einsum('xb,ybc->yxc', col_ops[level], stretched, precision=lax.Precision.HIGHEST)
    return merged

def reference(features, extents, canvas_large, label_mask, kernel_one, kernel_two, kernel_three, kernel_four, kernel_five, kernel_six, affine_scale, affine_shift, head_lower, head_upper, gain_lower, gain_upper, merged_grad):
    kernels = tuple((weight.astype(jnp.float32) for weight in (kernel_one, kernel_two, kernel_three, kernel_four, kernel_five, kernel_six)))
    heads = (head_lower.astype(jnp.float32), head_upper.astype(jnp.float32))
    gains = (gain_lower, gain_upper)
    stepper = jax.checkpoint(image_forward)

    def forward(image_all, kernel_set, head_set, gain_set):

        def one_image(item):
            return stepper(kernel_set, head_set, gain_set, affine_scale, affine_shift, item[0], item[1], item[2])
        return lax.map(one_image, (image_all, extents, canvas_large))
    merged, pullback = jax.vjp(forward, features.astype(jnp.float32), kernels, heads, gains)
    cotangent = merged_grad.astype(jnp.float32) * label_mask.astype(jnp.float32)[..., None]
    image_grad, kernel_grads, head_grads, gain_grads = pullback(cotangent)
    return (merged.astype(jnp.bfloat16), image_grad.astype(jnp.bfloat16), kernel_grads[0].reshape(-1), kernel_grads[1].reshape(-1), kernel_grads[2].reshape(-1), kernel_grads[3].reshape(-1), kernel_grads[4].reshape(-1), kernel_grads[5].reshape(-1), head_grads[0].reshape(-1), head_grads[1].reshape(-1), gain_grads[0], gain_grads[1])
```

```python
import functools

import jax
import jax.numpy as jnp
from jax import lax
from jax.experimental import pallas as pl
from jax.experimental.pallas import tpu as pltpu
from jax.sharding import PartitionSpec as P

C_MID = 512
TASKS = 7
TASK_C = 256
HEAD_OUT = 1792
CANVAS = 24
PIXELS = CANVAS * CANVAS
HALF = PIXELS // 2
DILATIONS = (1, 1, 1, 2, 2, 2)
EDGE = 48
SIDE = 8
VMEM_LIMIT = 56 << 20

BF16 = jnp.bfloat16
F32 = jnp.float32


def vmem():
    return pl.BlockSpec(memory_space=pltpu.VMEM)


def smem():
    return pl.BlockSpec(memory_space=pltpu.SMEM)


def hbm():
    return pl.BlockSpec(memory_space=pl.ANY)


def params():
    return pltpu.CompilerParams(vmem_limit_bytes=VMEM_LIMIT)


def cost(flops, moved):
    return pl.CostEstimate(flops=int(flops), bytes_accessed=int(moved), transcendentals=0)


def device_facts(extent, largest, own, core):
    height, breadth = extent[0], extent[1]
    big = (largest == own).astype(jnp.int32)
    return jnp.stack(
        [height, breadth, height // 2, breadth // 2, height // 4, breadth // 4, big, own, core]
    ).astype(jnp.int32)


def sources(facts):
    height, breadth, big = facts[0], facts[1], facts[6]
    place = jnp.arange(PIXELS, dtype=jnp.int32)
    row, col = place // CANVAS, place % CANVAS
    valid = (row < height) & (col < breadth)
    start_col = CANVAS // 2 + 2
    half = row * facts[2] // height * CANVAS + col * facts[3] // breadth
    quarter = row * facts[4] // height * CANVAS + start_col + col * facts[5] // breadth
    half = jnp.where(valid, half, -1)
    quarter = jnp.where(valid, quarter, -1)
    first = jnp.where(big == 1, jnp.where(valid, place, -1), half)
    second = jnp.where(big == 1, -1, quarter)
    return jnp.stack([first, second]), jnp.stack([half, quarter])


def pixel_mask(facts):
    place = lax.broadcasted_iota(jnp.int32, (PIXELS, 1), 0)
    row, col = place // CANVAS, place % CANVAS
    start_col = CANVAS // 2 + 2
    large = ((row < facts[0]) & (col < facts[1])).astype(F32)
    half = ((row < facts[2]) & (col < facts[3])).astype(F32)
    quarter = (
        (row < facts[4]) & (col >= start_col) & (col < start_col + facts[5])
    ).astype(F32)
    small = jnp.maximum(half, quarter)
    return jnp.where(facts[6] == 1, large, small)


def spread(values, pad, copies, base, dilation, flip):
    pad[SIDE : SIDE + PIXELS] = values
    col = lax.broadcasted_iota(jnp.int32, (PIXELS, 1), 0) % CANVAS
    for tap in range(3):
        shift = (1 - tap if flip else tap - 1) * dilation
        moved = pad[SIDE + shift : SIDE + shift + PIXELS]
        if shift != 0:
            inside = (col + shift >= 0) & (col + shift < CANVAS)
            moved = jnp.where(inside, moved, 0.0)
        copies[tap, base : base + PIXELS] = moved.astype(BF16)


def clear_edges(copies, base):
    width = copies.shape[2]
    for tap in range(3):
        copies[tap, base - EDGE : base] = jnp.zeros((EDGE, width), BF16)
        copies[tap, base + PIXELS : base + PIXELS + EDGE] = jnp.zeros((EDGE, width), BF16)


def tap_start(base, row_tap, dilation, flip):
    return base + (1 - row_tap if flip else row_tap - 1) * dilation * CANVAS


def forward_kernel(
    facts,
    features,
    scale,
    shift,
    w1,
    w2,
    w3,
    w4,
    w5,
    w6,
    e1,
    e2,
    e3,
    e4,
    e5,
    e6,
    top,
    g1,
    g2,
    g3,
    g4,
    g5,
    g6,
    weights,
    pad_in,
    pad,
    copies_in,
    copies,
    total,
    sems,
):
    kernels = (w1, w2, w3, w4, w5, w6)
    entered = (e1, e2, e3, e4, e5, e6, top)
    slopes = (g1, g2, g3, g4, g5, g6)

    def load(layer):
        rows = kernels[layer].shape[0]
        return pltpu.make_async_copy(
            kernels[layer], weights.at[layer % 2, pl.ds(0, rows)], sems.at[layer % 2]
        )

    load(0).start()
    load(1).start()
    mask = pixel_mask(facts)
    clear_edges(copies_in, EDGE)
    clear_edges(copies, EDGE)
    current = features[...].astype(F32) * mask
    e1[...] = current.astype(BF16)
    for layer in range(6):
        dilation = DILATIONS[layer]
        fan = kernels[layer].shape[0] // 9
        source = copies_in if layer == 0 else copies
        spread(current, pad_in if layer == 0 else pad, source, EDGE, dilation, False)
        load(layer).wait()
        for row_tap in range(3):
            begin = tap_start(EDGE, row_tap, dilation, False)
            for col_tap in range(3):
                tap = 3 * row_tap + col_tap
                part = jnp.dot(
                    source[col_tap, begin : begin + PIXELS],
                    weights[layer % 2, tap * fan : (tap + 1) * fan],
                    preferred_element_type=F32,
                )
                if tap == 0:
                    total[...] = part
                else:
                    total[...] += part
        if layer + 2 < 6:
            load(layer + 2).start()
        factor = scale[layer : layer + 1]
        h = total[...] * factor + shift[layer : layer + 1]
        root = 0.7978845608028654
        t = jnp.tanh(root * (h + 0.044715 * (h * h * h)))
        slope = 0.5 * (1.0 + t) + 0.5 * h * (1.0 - t * t) * (root * (1.0 + 0.134145 * (h * h)))
        slopes[layer][...] = (slope * factor * mask).astype(BF16)
        current = mask * (0.5 * h * (1.0 + t))
        entered[layer + 1][...] = current.astype(BF16)


def run_forward(facts, features, scale, shift, kernels):
    fan = features.shape[1]
    wide = jax.ShapeDtypeStruct((PIXELS, C_MID), BF16)
    rows = kernels[1].shape[0]
    flops = sum(2 * PIXELS * k.shape[0] * k.shape[1] for k in kernels)
    moved = sum(2 * k.size for k in kernels) + 14 * PIXELS * C_MID * 2
    out = pl.pallas_call(
        forward_kernel,
        out_shape=[jax.ShapeDtypeStruct((PIXELS, fan), BF16)] + [wide] * 12,
        in_specs=[smem(), vmem(), vmem(), vmem()] + [hbm()] * 6,
        out_specs=[vmem()] * 13,
        scratch_shapes=[
            pltpu.VMEM((2, rows, C_MID), BF16),
            pltpu.VMEM((PIXELS + 2 * SIDE, fan), F32),
            pltpu.VMEM((PIXELS + 2 * SIDE, C_MID), F32),
            pltpu.VMEM((3, PIXELS + 2 * EDGE, fan), BF16),
            pltpu.VMEM((3, PIXELS + 2 * EDGE, C_MID), BF16),
            pltpu.VMEM((PIXELS, C_MID), F32),
            pltpu.SemaphoreType.DMA((2,)),
        ],
        compiler_params=params(),
        cost_estimate=cost(flops, moved),
        name="trunk_forward",
    )(facts, features, scale, shift, *kernels)
    return out[:6], out[6], out[7:]


def select_matrix(index, length, width):
    place = lax.broadcasted_iota(jnp.int32, (length, width), 0)
    hit = (place == index[0:1]).astype(F32) + (place == index[1:2]).astype(F32)
    return hit.astype(BF16)


def head_kernel(
    split,
    facts,
    index,
    grad_own,
    grad_other,
    taps,
    head,
    gain,
    *rest,
):
    if len(rest) == 9:
        before, out, keep, send, gain_grad, tap_grad, picks, grads, block = rest
    else:
        before = None
        out, keep, send, gain_grad, tap_grad, picks, grads, block = rest
    step = pl.program_id(0)

    @pl.when(step == 0)
    def _():
        picks[...] = select_matrix(index, PIXELS, PIXELS)

    own = facts[7]
    grads[pl.ds(pl.multiple_of(own * HALF, HALF), HALF)] = grad_own[...]
    grads[pl.ds(pl.multiple_of((1 - own) * HALF, HALF), HALF)] = grad_other[...]
    canvas_grad = jnp.dot(picks[...], grads[...], preferred_element_type=F32)
    project = jnp.dot(taps[...], head[...], preferred_element_type=F32)
    inverse = lax.rsqrt(jnp.sum(project * project, axis=1, keepdims=True) + 1e-06)
    normed = project * inverse
    factor = gain[0]
    made = (normed * factor).astype(BF16)
    if before is None:
        out[...] = made
    else:
        out[...] = (made.astype(F32) + before[...].astype(F32)).astype(BF16)
    product = canvas_grad * normed
    gain_grad[0] = jnp.sum(product, axis=0, keepdims=True)
    inner = jnp.sum(product * factor, axis=1, keepdims=True)
    dproject = ((canvas_grad * factor - normed * inner) * inverse).astype(BF16)
    weight_grad = lax.dot_general(
        taps[...], dproject, (((0,), (0,)), ((), ())), preferred_element_type=F32
    ).astype(BF16)
    if split is None:
        keep[...] = weight_grad
    else:
        bit = facts[8]
        block[...] = weight_grad
        for run in range(C_MID // (2 * split)):
            keep[run * split : (run + 1) * split] = block[
                pl.ds(pl.multiple_of((2 * run + bit) * split, split), split)
            ]
            send[run * split : (run + 1) * split] = block[
                pl.ds(pl.multiple_of((2 * run + 1 - bit) * split, split), split)
            ]
    back = lax.dot_general(
        dproject, head[...], (((1,), (1,)), ((), ())), preferred_element_type=F32
    )

    @pl.when(step == 0)
    def _():
        tap_grad[...] = back

    @pl.when(step > 0)
    def _():
        tap_grad[...] += back


def run_head(facts, index, grad_own, grad_other, taps, head, gain, before, split):
    if split is not None and split % 16:
        split = None
    kept = C_MID if split is None else C_MID // 2
    tile = lambda rows: pl.BlockSpec((rows, TASK_C), lambda i: (0, i))
    whole = lambda shape: pl.BlockSpec(shape, lambda i: (0, 0))
    gain_spec = pl.BlockSpec((1, 1, TASK_C), lambda i: (i, 0, 0))
    ins = [facts, index, grad_own, grad_other, taps, head, gain.reshape(TASKS, 1, TASK_C)]
    in_specs = [
        smem(),
        whole((2, PIXELS)),
        tile(HALF),
        tile(HALF),
        whole((PIXELS, C_MID)),
        tile(C_MID),
        gain_spec,
    ]
    if before is not None:
        ins.append(before)
        in_specs.append(tile(PIXELS))
    out, keep, send, gain_grad, tap_grad = pl.pallas_call(
        functools.partial(head_kernel, split),
        grid=(TASKS,),
        out_shape=[
            jax.ShapeDtypeStruct((PIXELS, HEAD_OUT), BF16),
            jax.ShapeDtypeStruct((kept, HEAD_OUT), BF16),
            jax.ShapeDtypeStruct((kept, HEAD_OUT), BF16),
            jax.ShapeDtypeStruct((TASKS, 1, TASK_C), F32),
            jax.ShapeDtypeStruct((PIXELS, C_MID), F32),
        ],
        in_specs=in_specs,
        out_specs=[
            tile(PIXELS),
            tile(kept),
            tile(kept),
            gain_spec,
            whole((PIXELS, C_MID)),
        ],
        scratch_shapes=[
            pltpu.VMEM((PIXELS, PIXELS), BF16),
            pltpu.VMEM((PIXELS, TASK_C), BF16),
            pltpu.VMEM((C_MID, TASK_C), BF16),
        ],
        compiler_params=params(),
        cost_estimate=cost(
            2 * PIXELS * HEAD_OUT * (3 * C_MID + PIXELS), 4 * PIXELS * HEAD_OUT + 8 * C_MID * HEAD_OUT
        ),
        name="heads",
    )(*ins)
    if split is None:
        send = None
    return out, keep, send, gain_grad.reshape(HEAD_OUT), tap_grad


def merge_kernel(facts, index, own, other, out):
    big = facts[6]
    start = pl.multiple_of(facts[7] * HALF, HALF)
    picks = select_matrix(index, HALF, HALF)

    @pl.when(big == 1)
    def _():
        read = lax.dot_general(
            picks, other[...], (((0,), (0,)), ((), ())), preferred_element_type=F32
        )
        out[...] = (read + own[pl.ds(start, HALF)].astype(F32)).astype(BF16)

    @pl.when(big == 0)
    def _():
        read = lax.dot_general(
            picks, own[0:HALF], (((0,), (0,)), ((), ())), preferred_element_type=F32
        )
        out[...] = (read + other[...].astype(F32)).astype(BF16)


def run_merge(facts, index, own, other):
    tile = lambda rows: pl.BlockSpec((rows, TASK_C), lambda i: (0, i))
    return pl.pallas_call(
        merge_kernel,
        grid=(TASKS,),
        out_shape=jax.ShapeDtypeStruct((HALF, HEAD_OUT), BF16),
        in_specs=[
            smem(),
            pl.BlockSpec((2, HALF), lambda i: (0, 0)),
            tile(PIXELS),
            tile(HALF),
        ],
        out_specs=tile(HALF),
        compiler_params=params(),
        cost_estimate=cost(2 * HALF * HALF * HEAD_OUT, 8 * HALF * HEAD_OUT),
        name="merge",
    )(facts, index, own, other)


def backward_kernel(dilation, final, extra, facts, weights_hbm, slope, grad, *rest):
    if extra:
        more, *rest = rest
    if final:
        own_half, other_half, back, weights, pad, copies, total, sems = rest
    else:
        own_half, other_half, back, weights, pad, copies, sems = rest
        total = back
    fan = weights_hbm.shape[0] // 9

    def load(tap):
        return pltpu.make_async_copy(
            weights_hbm.at[pl.ds(tap * fan, fan)], weights.at[pl.ds(tap * fan, fan)], sems.at[tap]
        )

    for tap in range(9):
        load(tap).start()
    clear_edges(copies, EDGE)
    dlinear = grad[...]
    if extra:
        dlinear = dlinear + more[...]
    dlinear = dlinear * slope[...].astype(F32)
    rounded = dlinear.astype(BF16)
    low, high = rounded[:, : C_MID // 2], rounded[:, C_MID // 2 :]
    first = facts[8] == 0
    own_half[...] = jnp.where(first, low, high)
    other_half[...] = jnp.where(first, high, low)
    spread(dlinear, pad, copies, EDGE, dilation, True)
    for row_tap in range(3):
        begin = tap_start(EDGE, row_tap, dilation, True)
        for col_tap in range(3):
            tap = 3 * row_tap + col_tap
            load(tap).wait()
            part = lax.dot_general(
                copies[col_tap, begin : begin + PIXELS],
                weights[tap * fan : (tap + 1) * fan],
                (((1,), (1,)), ((), ())),
                preferred_element_type=F32,
            )
            if tap == 0:
                total[...] = part
            else:
                total[...] += part
    if final:
        back[...] = (total[...] * pixel_mask(facts)).astype(BF16)


def run_backward(depth, facts, weights, slope, grad, more):
    rows = weights.shape[0]
    fan = rows // 9
    final = depth == 0
    extra = more is not None
    half = jax.ShapeDtypeStruct((PIXELS, C_MID // 2), BF16)
    scratch = [
        pltpu.VMEM((rows, C_MID), BF16),
        pltpu.VMEM((PIXELS + 2 * SIDE, C_MID), F32),
        pltpu.VMEM((3, PIXELS + 2 * EDGE, C_MID), BF16),
    ]
    if final:
        scratch.append(pltpu.VMEM((PIXELS, fan), F32))
    scratch.append(pltpu.SemaphoreType.DMA((9,)))
    return pl.pallas_call(
        functools.partial(backward_kernel, DILATIONS[depth], final, extra),
        out_shape=[half, half, jax.ShapeDtypeStruct((PIXELS, fan), BF16 if final else F32)],
        in_specs=[smem(), hbm(), vmem(), vmem()] + [vmem()] * extra,
        out_specs=[vmem()] * 3,
        scratch_shapes=scratch,
        compiler_params=params(),
        cost_estimate=cost(2 * PIXELS * rows * C_MID, 2 * rows * C_MID + 12 * PIXELS * C_MID),
        name="input_gradient",
    )(facts, weights, slope, grad, *([more] if extra else []))


def weight_kernel(dilation, split, bit_ref, mine, theirs, grad_mine, grad_theirs, *rest):
    if split is None:
        out, pads, copies, both = rest
        made = out
    else:
        keep, send, pads, copies, both, made = rest
    fan = mine.shape[1]
    width = grad_mine.shape[1]
    second = 2 * EDGE + PIXELS + EDGE
    clear_edges(copies, EDGE)
    clear_edges(copies, second)
    spread(grad_mine[...].astype(F32), pads, copies, EDGE, dilation, True)
    spread(grad_theirs[...].astype(F32), pads, copies, second, dilation, True)
    both[0:PIXELS] = mine[...]
    both[PIXELS : 2 * PIXELS] = theirs[...]
    for row_tap in range(3):
        begin = tap_start(EDGE, row_tap, dilation, True)
        later = tap_start(second, row_tap, dilation, True)
        for col_tap in range(3):
            tap = 3 * row_tap + col_tap
            shifted = jnp.concatenate(
                [copies[col_tap, begin : begin + PIXELS], copies[col_tap, later : later + PIXELS]],
                axis=0,
            )
            made[tap * fan : (tap + 1) * fan] = lax.dot_general(
                both[...], shifted, (((0,), (0,)), ((), ())), preferred_element_type=F32
            ).astype(BF16)
    if split is not None:
        bit = bit_ref[0]
        for run in range(9 * fan // (2 * split)):
            keep[run * split : (run + 1) * split] = made[
                pl.ds(pl.multiple_of((2 * run + bit) * split, split), split)
            ]
            send[run * split : (run + 1) * split] = made[
                pl.ds(pl.multiple_of((2 * run + 1 - bit) * split, split), split)
            ]


def run_weight(depth, bit, mine, theirs, grad_mine, grad_theirs, split):
    if split % 16:
        split = None
    fan = mine.shape[1]
    width = grad_mine.shape[1]
    rows = 9 * fan
    scratch = [
        pltpu.VMEM((PIXELS + 2 * SIDE, width), F32),
        pltpu.VMEM((3, 2 * PIXELS + 4 * EDGE, width), BF16),
        pltpu.VMEM((2 * PIXELS, fan), BF16),
    ]
    if split is None:
        outs = [jax.ShapeDtypeStruct((rows, width), BF16)]
    else:
        outs = [jax.ShapeDtypeStruct((rows // 2, width), BF16)] * 2
        scratch.append(pltpu.VMEM((rows, width), BF16))
    made = pl.pallas_call(
        functools.partial(weight_kernel, DILATIONS[depth], split),
        out_shape=outs,
        in_specs=[smem()] + [vmem()] * 4,
        out_specs=[vmem()] * len(outs),
        scratch_shapes=scratch,
        compiler_params=params(),
        cost_estimate=cost(4 * PIXELS * rows * width, 2 * rows * width + 4 * PIXELS * (fan + width)),
        name="weight_gradient",
    )(bit.reshape(1), mine, theirs, grad_mine, grad_theirs)
    return made[0], (None if split is None else made[1])


def exchange(array, name):
    if name == "scale":
        return lax.ppermute(array, "scale", [(0, 1), (1, 0)])
    count = lax.axis_size("img")
    return lax.ppermute(array, "img", [(i, i ^ (1 << name)) for i in range(count)])


def own_bit(name):
    if name == "scale":
        return lax.axis_index("scale")
    return (lax.axis_index("img") >> name) & 1


def pick(array, which, axis):
    return lax.dynamic_index_in_dim(array, which, axis, keepdims=False)


def bits():
    return lax.axis_size("img").bit_length() - 1


def run_length(rows, name):
    block = rows // (lax.axis_size("img") * lax.axis_size("scale"))
    return block if name == "scale" else block * 2 << name


def orders(first):
    near = [1, "scale"] + list(range(2, bits()))
    near.remove(first)
    return [first] + near


def reduce_rows(keep, send, rows, order):
    names = list(reversed(range(bits()))) + ["scale"]
    block = rows // (2 ** len(names))
    width = keep.shape[-1]
    if send is None:
        axis = names.index(order[0])
        whole = keep.reshape((2,) * len(names) + (block, width))
        bit = own_bit(order[0])
        keep, send = pick(whole, bit, axis), pick(whole, 1 - bit, axis)
    names.remove(order[0])
    shape = (2,) * len(names) + (block, width)
    keep = keep.reshape(shape)
    came = exchange(send, order[0]).reshape(shape)
    for name in order[1:]:
        axis = names.index(name)
        bit = own_bit(name)
        send = (
            pick(keep, 1 - bit, axis).astype(F32) + pick(came, 1 - bit, axis).astype(F32)
        ).astype(BF16)
        keep = (pick(keep, bit, axis).astype(F32) + pick(came, bit, axis).astype(F32)).astype(BF16)
        came = exchange(send, name)
        names.remove(name)
    return keep.astype(F32) + came.astype(F32)


def join_columns(summed):
    core = own_bit(0)
    mine = pick(summed, core, 0)
    other = exchange(pick(summed, 1 - core, 0), 0)
    left = jnp.where(core == 0, mine, other)
    right = jnp.where(core == 0, other, mine)
    return jnp.concatenate([left, right], axis=1).reshape(-1)


def on_device(
    features,
    extents,
    canvas_large,
    label_mask,
    kernel_one,
    kernel_two,
    kernel_three,
    kernel_four,
    kernel_five,
    kernel_six,
    affine_scale,
    affine_shift,
    head_lower,
    head_upper,
    gain_lower,
    gain_upper,
    merged_grad,
):
    kernels = (kernel_one, kernel_two, kernel_three, kernel_four, kernel_five, kernel_six)
    own = lax.axis_index("scale")
    facts = device_facts(extents[0], canvas_large[0], own, own_bit(0))
    index, small_index = sources(facts)
    small_index = lax.dynamic_slice_in_dim(small_index, own * HALF, HALF, 1)

    grad_own = (merged_grad * label_mask[..., None].astype(BF16)).reshape(HALF, HEAD_OUT)
    grad_other = exchange(grad_own, "scale")

    entered, top, slopes = run_forward(
        facts, features.reshape(PIXELS, -1), affine_scale, affine_shift, kernels
    )
    partner = [exchange(e, 0) for e in entered]

    head_split = run_length(C_MID, 0)
    lower, keep_lower, send_lower, gain_lower_grad, back_lower = run_head(
        facts, index, grad_own, grad_other, entered[3], head_lower, gain_lower, None, head_split
    )
    summed_taps, keep_upper, send_upper, gain_upper_grad, back = run_head(
        facts, index, grad_own, grad_other, top, head_upper, gain_upper, lower, head_split
    )
    start = jnp.where(facts[6] == 1, (1 - own) * HALF, 0)
    taps_other = exchange(lax.dynamic_slice_in_dim(summed_taps, start, HALF, 0), "scale")
    merged = run_merge(facts, small_index, summed_taps, taps_other)

    order = [0] + orders(1)
    head_lower_grad = reduce_rows(keep_lower, send_lower, C_MID, order).reshape(-1)
    head_upper_grad = reduce_rows(keep_upper, send_upper, C_MID, order).reshape(-1)

    gains = lax.psum(jnp.stack([gain_lower_grad, gain_upper_grad]), ("img", "scale"))
    share = HEAD_OUT // (lax.axis_size("img") * lax.axis_size("scale"))
    place = lax.axis_index("img") * lax.axis_size("scale") + own
    gains = lax.dynamic_slice_in_dim(gains, place * share, share, 1)

    firsts = (1, "scale", 2, 1, "scale", 1)
    kernel_grads = [None] * 6
    for depth in reversed(range(6)):
        mine, other, back = run_backward(
            depth, facts, kernels[depth], slopes[depth], back, back_lower if depth == 2 else None
        )
        theirs = exchange(other, 0)
        first = firsts[depth]
        rows = kernels[depth].shape[0]
        keep, send = run_weight(
            depth,
            own_bit(first),
            entered[depth],
            partner[depth],
            mine,
            theirs,
            run_length(rows, first),
        )
        summed = reduce_rows(keep, send, rows, orders(first))
        kernel_grads[depth] = join_columns(summed)
    features_grad = back.reshape(features.shape)
    return (
        merged.reshape(merged_grad.shape),
        features_grad,
        *kernel_grads,
        head_lower_grad,
        head_upper_grad,
        gains[0],
        gains[1],
    )


def solution(mesh):
    in_specs = (
        P("img", "scale", None, None, None),
        P("img", None),
        P("img"),
        P("img", "scale", None),
        P(),
        P(),
        P(),
        P(),
        P(),
        P(),
        P(),
        P(),
        P(),
        P(),
        P(),
        P(),
        P("img", "scale", None, None),
    )
    out_specs = (
        P("img", "scale", None, None),
        P("img", "scale", None, None, None),
        P(("img", "scale")),
        P(("img", "scale")),
        P(("img", "scale")),
        P(("img", "scale")),
        P(("img", "scale")),
        P(("img", "scale")),
        P(("img", "scale")),
        P(("img", "scale")),
        P(("img", "scale")),
        P(("img", "scale")),
    )
    return jax.shard_map(
        on_device, mesh=mesh, in_specs=in_specs, out_specs=out_specs, check_vma=False
    )
```

```python
import functools

import jax
import jax.numpy as jnp
from jax import lax
from jax.experimental import pallas as pl
from jax.experimental.pallas import tpu as pltpu
from jax.sharding import PartitionSpec as P

C_MID = 512
TASKS = 7
TASK_C = 256
HEAD_OUT = 1792
CANVAS = 24
PIXELS = CANVAS * CANVAS
HALF = PIXELS // 2
DILATIONS = (1, 1, 1, 2, 2, 2)
EDGE = 48
SIDE = 8
WIDTH = 256
MEGABYTES = 63
START_COL = CANVAS // 2 + 2

BF16 = jnp.bfloat16
F32 = jnp.float32

SMEM = pl.BlockSpec(memory_space=pltpu.SMEM)
HBM = pl.BlockSpec(memory_space=pltpu.HBM)
VMEM = pl.BlockSpec(memory_space=pltpu.VMEM)


def shape(rows, width, kind=BF16):
    return jax.ShapeDtypeStruct((rows, width), kind)


def buffer(rows, width, kind=BF16):
    return pltpu.VMEM((rows, width), kind)


def aligned(index):
    return pl.multiple_of(index, 16)


def bits():
    return lax.axis_size("img").bit_length() - 1


def own_bit(name):
    if name == "scale":
        return lax.axis_index("scale")
    return (lax.axis_index("img") >> name) & 1


def mark(name):
    return 0 if name == "scale" else 1 + name


def exchange(array, name):
    if name == "scale":
        return lax.ppermute(array, "scale", [(0, 1), (1, 0)])
    count = lax.axis_size("img")
    return lax.ppermute(array, "img", [(i, i ^ (1 << name)) for i in range(count)])


class Chain:
    def __init__(self, copies, rows, width=WIDTH):
        self.width = width
        self.names = list(reversed(range(bits()))) + ["scale"]
        self.block = rows // (2 ** len(self.names))
        self.copies = copies
        self.keep = self.came = None

    def rows(self):
        return self.copies * self.block * 2 ** len(self.names)

    def run(self, name):
        return self.block * 2 ** (len(self.names) - 1 - self.names.index(name))

    def remove(self, name, keep, came):
        self.names.remove(name)
        self.keep, self.came = keep, came


def rows_of(piece, rows):
    array, first = piece
    return lax.slice_in_dim(array, first, first + rows, axis=0)


class Totals(Chain):
    def __init__(self, keep):
        self.names = list(reversed(range(bits()))) + ["scale"]
        self.width = keep.shape[1]
        self.count = keep.shape[0]
        self.keep = (keep, 0)

    def rows(self):
        return self.count

    def run(self, name):
        return self.count

    def split(self, total):
        high = total.astype(BF16)
        return high, (total - high.astype(F32)).astype(BF16)

    def add(self, mine, theirs):
        half = self.count // 2
        total = mine[:half].astype(F32) + theirs[:half].astype(F32)
        return self.split(total + (mine[half:].astype(F32) + theirs[half:].astype(F32)))


class Step:
    def __init__(self, name, *chains):
        self.name, self.chains = name, chains
        self.width = WIDTH
        self.sizes = [(chain.rows(), chain.run(name)) for chain in chains]
        self.fits = all(run % 16 == 0 for _, run in self.sizes)
        self.left = [rows if isinstance(c, Totals) else rows // 2 for c, (rows, _) in zip(chains, self.sizes)]
        self.total = sum(self.left)

    def plain(self):
        bit = own_bit(self.name)
        keeps, sends = [], []
        for chain, (rows, run) in zip(self.chains, self.sizes):
            if isinstance(chain, Totals):
                both = jnp.concatenate(
                    chain.add(rows_of(chain.keep, rows), rows_of(chain.came, rows))
                )
                keeps.append(both)
                sends.append(both)
                continue
            both = rows_of(chain.keep, rows).astype(F32) + rows_of(chain.came, rows).astype(F32)
            both = both.astype(BF16).reshape(rows // (2 * run), 2, run, self.width)
            choose = lambda which: lax.dynamic_index_in_dim(both, which, 1, keepdims=False)
            keeps.append(choose(bit).reshape(rows // 2, self.width))
            sends.append(choose(1 - bit).reshape(rows // 2, self.width))
        return keeps, jnp.concatenate(sends) if len(sends) > 1 else sends[0]

    def done(self, keeps, send):
        came, first = exchange(send, self.name), 0
        for chain, keep, left in zip(self.chains, keeps, self.left):
            chain.remove(self.name, (keep, 0), (came, first))
            first += left

    def go(self):
        self.done(*self.plain())

    def operands(self):
        return [part[0] for chain in self.chains for part in (chain.keep, chain.came)]

    def outs(self):
        return [shape(left, self.width) for left in [*self.left, self.total]]

    def scratch(self):
        made = [buffer(rows, self.width) for rows, _ in self.sizes for _ in range(2)]
        count = 2 * len(self.sizes)
        return made + [pltpu.SemaphoreType.DMA((count,)), pltpu.SemaphoreType.DMA((count,))]

    def bind(self, marks, ins, outs, scratch):
        bit = marks[mark(self.name)]
        in_sems, out_sems = scratch[-2], scratch[-1]
        loads, stores, sums = [], [], []
        sent = 0
        for place, (chain, left, (rows, run)) in enumerate(
            zip(self.chains, self.left, self.sizes)
        ):
            mine, theirs = scratch[2 * place], scratch[2 * place + 1]
            loads.append((ins[2 * place].at[pl.ds(chain.keep[1], rows)], mine))
            loads.append((ins[2 * place + 1].at[pl.ds(chain.came[1], rows)], theirs))
            there = outs[-1].at[pl.ds(sent, left)]
            sent += left
            if isinstance(chain, Totals):
                sums.append((chain, mine, theirs))
                stores += [(mine, outs[place]), (mine, there)]
                continue
            pairs = rows // (2 * run)
            view = lambda ref, pairs=pairs, run=run: ref.reshape(pairs, 2, run, self.width)
            part = lambda ref, pairs=pairs, run=run: ref.reshape(pairs, run, self.width)
            sums.append((None, view(mine), view(theirs)))
            stores.append((view(mine).at[:, bit], part(outs[place])))
            stores.append((view(theirs).at[:, 1 - bit], part(there)))

        def load():
            return [pltpu.make_async_copy(*one, in_sems.at[i]) for i, one in enumerate(loads)]

        def store():
            return [pltpu.make_async_copy(*one, out_sems.at[i]) for i, one in enumerate(stores)]

        def begin():
            for one in load():
                one.start()

        def work():
            for one in load():
                one.wait()
            for chain, mine, theirs in sums:
                if chain is None:
                    mine[:, bit] = mine[:, bit] + theirs[:, bit]
                    theirs[:, 1 - bit] = mine[:, 1 - bit] + theirs[:, 1 - bit]
                else:
                    half = chain.count // 2
                    high, low = chain.add(mine[...], theirs[...])
                    mine[0:half] = high
                    mine[half:] = low
            for one in store():
                one.start()

        def finish():
            for one in store():
                one.wait()

        return begin, work, finish


class Ride:
    def __init__(self, parts):
        self.parts = parts

    def begin(self):
        for begin, _, _ in self.parts:
            begin()

    def work(self):
        for _, work, _ in self.parts:
            work()

    def finish(self):
        for _, _, finish in self.parts:
            finish()


def kernel_call(
    kernel, name, marks, ins, in_specs, outs, out_specs, scratch, flops, after, steps, grid=(), weight=0.3, aliases=()
):
    after = list(after)
    steps = [step for step in steps if step.chains]
    riders = [step for step in steps if step.fits]
    for step in steps:
        if not step.fits:
            keeps, send = step.plain()
            step.done(keeps, send)
            after.append(send)
    ride_ins = [step.operands() for step in riders]
    ride_outs = [step.outs() for step in riders]
    ride_scratch = [step.scratch() for step in riders]
    flat = lambda lists: [one for part in lists for one in part]

    def body(*refs):
        refs = list(refs)

        def take(count):
            taken = refs[:count]
            del refs[:count]
            return taken

        take(len(after))
        (marks_ref,) = take(1)
        r_ins = [take(len(part)) for part in ride_ins]
        used = take(len(ins) + len(outs))
        r_outs = [take(len(part)) for part in ride_outs]
        own = take(len(scratch))
        r_scratch = [take(len(part)) for part in ride_scratch]
        ride = Ride(
            [
                step.bind(marks_ref, *refs3)
                for step, *refs3 in zip(riders, r_ins, r_outs, r_scratch)
            ]
        )
        kernel(ride, marks_ref, *used, *own)

    results = pl.pallas_call(
        body,
        grid=grid,
        out_shape=[*outs, *flat(ride_outs)],
        in_specs=[HBM] * len(after) + [SMEM] + [HBM] * len(flat(ride_ins)) + in_specs,
        out_specs=[*out_specs] + [HBM] * len(flat(ride_outs)),
        scratch_shapes=[*scratch, *flat(ride_scratch)],
        compiler_params=pltpu.CompilerParams(vmem_limit_bytes=MEGABYTES << 20),
        cost_estimate=pl.CostEstimate(
            flops=int(weight * flops), bytes_accessed=1 << 20, transcendentals=0
        ),
        input_output_aliases={
            len(after) + 1 + len(flat(ride_ins)) + one: other for one, other in aliases
        },
        name=name,
    )(*after, marks, *flat(ride_ins), *ins)
    made, rest = list(results[: len(outs)]), list(results[len(outs) :])
    for step, part in zip(riders, ride_outs):
        *keeps, send = rest[: len(part)]
        del rest[: len(part)]
        step.done(keeps, send)
    return made


class Place:
    def __init__(self, marks, extents, largest):
        self.height, self.breadth = extents[0, 0], extents[0, 1]
        self.own, self.core = marks[0], marks[1]
        self.big = largest[0] == self.own


def scaled(place, extent, level):
    product = (place * (extent >> level)).astype(F32) + 0.5
    return jnp.floor(product / extent.astype(F32)).astype(jnp.int32)


def sources(place, offset, count):
    spot = lax.broadcasted_iota(jnp.int32, (1, count), 1) + offset
    row, col = spot // CANVAS, spot % CANVAS
    valid = (row < place.height) & (col < place.breadth)
    half = scaled(row, place.height, 1) * CANVAS + scaled(col, place.breadth, 1)
    quarter = scaled(row, place.height, 2) * CANVAS + START_COL + scaled(col, place.breadth, 2)
    return jnp.where(valid, half, -1), jnp.where(valid, quarter, -1), jnp.where(valid, spot, -1)


def select_matrix(first, second, length):
    spot = lax.broadcasted_iota(jnp.int32, (length, first.shape[1]), 0)
    return ((spot == first).astype(F32) + (spot == second).astype(F32)).astype(BF16)


def pixel_mask(place):
    spot = lax.broadcasted_iota(jnp.int32, (PIXELS, 1), 0)
    row, col = spot // CANVAS, spot % CANVAS
    height, breadth = place.height, place.breadth
    large = ((row < height) & (col < breadth)).astype(F32)
    half = ((row < height >> 1) & (col < breadth >> 1)).astype(F32)
    quarter = (
        (row < height >> 2) & (col >= START_COL) & (col < START_COL + (breadth >> 2))
    ).astype(F32)
    return jnp.where(place.big, large, jnp.maximum(half, quarter))


def spread(values, pad, copies, base, dilation, flip, taps=(0, 1, 2)):
    if values is not None:
        pad[SIDE : SIDE + PIXELS] = values
    col = lax.broadcasted_iota(jnp.int32, (PIXELS, 1), 0) % CANVAS
    for tap in taps:
        shift = (1 - tap if flip else tap - 1) * dilation
        moved = pad[SIDE + shift : SIDE + shift + PIXELS]
        if shift != 0:
            inside = (col + shift >= 0) & (col + shift < CANVAS)
            moved = jnp.where(inside, moved, 0.0)
        copies[tap, base : base + PIXELS] = moved.astype(BF16)


def clear_edges(copies, base):
    width = copies.shape[2]
    for tap in range(3):
        copies[tap, base - EDGE : base] = jnp.zeros((EDGE, width), BF16)
        copies[tap, base + PIXELS : base + PIXELS + EDGE] = jnp.zeros((EDGE, width), BF16)


def tap_start(base, row_tap, dilation, flip):
    return base + (1 - row_tap if flip else row_tap - 1) * dilation * CANVAS


def forward_kernel(
    ride,
    marks,
    extents,
    largest,
    features,
    scale_hbm,
    shift_hbm,
    w1,
    w2,
    w3,
    w4,
    w5,
    w6,
    entered,
    top,
    g1,
    g2,
    g3,
    g4,
    g5,
    g6,
    weights,
    first,
    scale,
    shift,
    pad_in,
    pad,
    copies_in,
    copies,
    total,
    made_e,
    made_g,
    sems,
    out_sems,
    small_sems,
):
    kernels = (w1, w2, w3, w4, w5, w6)
    slopes = (g1, g2, g3, g4, g5, g6)
    copy = pltpu.make_async_copy

    def load(layer):
        rows = kernels[layer].shape[0]
        return copy(kernels[layer], weights.at[layer % 2, pl.ds(0, rows)], sems.at[layer % 2])

    def store_e(layer):
        there = top if layer == 6 else entered.at[pl.ds(layer * PIXELS, PIXELS)]
        return copy(made_e.at[layer % 2], there, out_sems.at[0, layer % 2])

    def store_g(layer):
        return copy(made_g.at[layer % 2], slopes[layer], out_sems.at[1, layer % 2])

    small = [
        copy(features, first, small_sems.at[0]),
        copy(scale_hbm, scale, small_sems.at[1]),
        copy(shift_hbm, shift, small_sems.at[2]),
    ]
    for one in small:
        one.start()
    load(0).start()
    mask = pixel_mask(Place(marks, extents, largest))
    clear_edges(copies_in, EDGE)
    clear_edges(copies, EDGE)
    for one in small:
        one.wait()
    fan = features.shape[1]
    current = first[...].astype(F32) * mask
    made_e[0] = jnp.zeros_like(made_e[0])
    made_e[0, :, 0:fan] = current.astype(BF16)
    store_e(0).start()
    for layer in range(6):
        dilation = DILATIONS[layer]
        fan = kernels[layer].shape[0] // 9
        source = copies_in if layer == 0 else copies
        spread(current, pad_in if layer == 0 else pad, source, EDGE, dilation, False)
        load(layer).wait()
        if layer + 1 < 6:
            load(layer + 1).start()
        for row_tap in range(3):
            begin = tap_start(EDGE, row_tap, dilation, False)
            for col_tap in range(3):
                tap = 3 * row_tap + col_tap
                part = jnp.dot(
                    source[col_tap, begin : begin + PIXELS],
                    weights[layer % 2, tap * fan : (tap + 1) * fan],
                    preferred_element_type=F32,
                )
                if tap == 0:
                    total[...] = part
                else:
                    total[...] += part
        factor = scale[layer : layer + 1]
        h = total[...] * factor + shift[layer : layer + 1]
        root = 0.7978845608028654
        square = h * h
        t = jnp.tanh(h * (root + 0.044715 * root * square))
        rise = 0.5 + 0.5 * t
        current = h * rise
        slope = rise + (current - current * t) * (root + 0.134145 * root * square)
        if layer >= 2:
            store_g(layer - 2).wait()
        if layer >= 1:
            store_e(layer - 1).wait()
        made_g[layer % 2] = (slope * (factor * mask)).astype(BF16)
        current = mask * current
        made_e[(layer + 1) % 2] = current.astype(BF16)
        store_e(layer + 1).start()
        store_g(layer).start()
    for layer in (4, 5):
        store_e(layer + 1).wait()
        store_g(layer).wait()


def run_forward(marks, facts, features, scale, shift, kernels, after):
    fan = features.shape[1]
    rows = kernels[1].shape[0]
    entered, top, *slopes = kernel_call(
        forward_kernel,
        "trunk_forward",
        marks,
        [*facts, features, scale, shift, *kernels],
        [SMEM] * 2 + [HBM] * 9,
        [shape(6 * PIXELS, C_MID)] + [shape(PIXELS, C_MID)] * 7,
        [HBM] * 8,
        [
            pltpu.VMEM((2, rows, C_MID), BF16),
            buffer(PIXELS, fan),
            buffer(6, C_MID, F32),
            buffer(6, C_MID, F32),
            buffer(PIXELS + 2 * SIDE, fan, F32),
            buffer(PIXELS + 2 * SIDE, C_MID, F32),
            pltpu.VMEM((3, PIXELS + 2 * EDGE, fan), BF16),
            pltpu.VMEM((3, PIXELS + 2 * EDGE, C_MID), BF16),
            buffer(PIXELS, C_MID, F32),
            pltpu.VMEM((2, PIXELS, C_MID), BF16),
            pltpu.VMEM((2, PIXELS, C_MID), BF16),
            pltpu.SemaphoreType.DMA((2,)),
            pltpu.SemaphoreType.DMA((2, 2)),
            pltpu.SemaphoreType.DMA((3,)),
        ],
        sum(2 * PIXELS * k.size for k in kernels),
        after,
        [],
        weight=2.5,
    )
    return entered, top, slopes


def head_chain(project, canvas_grad, factor):
    inverse = lax.rsqrt(jnp.sum(project * project, axis=1, keepdims=True) + 1e-06)
    made = (project * inverse * factor).astype(BF16)
    scaled_grad = canvas_grad * inverse
    product = scaled_grad * project
    gain_grad = jnp.sum(product, axis=0, keepdims=True)
    inner = jnp.sum(product * factor, axis=1, keepdims=True) * (inverse * inverse)
    return made, (scaled_grad * factor - project * inner).astype(BF16), gain_grad


def head_kernel(split, ride, marks, extents, largest, grad_own, grad_other, *rest):
    taps, heads, gains = rest[0:2], rest[2:4], rest[4:6]
    out, send_out, _, *rest = rest[6:]
    if split:
        keeps, sends, rest = rest[0:2], rest[2:4], rest[4:]
    else:
        keeps, sends, rest = rest[0:2], None, rest[2:]
    gain_grads, tap_grads, rest = rest[0:2], rest[2:4], rest[4:]
    picks, grads, block, *turned = rest
    step = pl.program_id(0)
    place = Place(marks, extents, largest)
    own = place.own

    @pl.when(step == 0)
    def _():
        ride.begin()
        half, quarter, same = sources(place, 0, PIXELS)
        picks[...] = select_matrix(
            jnp.where(place.big, same, half), jnp.where(place.big, -1, quarter), PIXELS
        )
        for i in range(2):
            turned[i][...] = taps[i][...].T

    def some_heads(count):
        wide = slice(0, count * TASK_C)
        grads[pl.ds(aligned(own * HALF), HALF), wide] = grad_own[:, wide]
        grads[pl.ds(aligned((1 - own) * HALF), HALF), wide] = grad_other[:, wide]
        projects = [
            jnp.dot(taps[i][...], heads[i][:, wide], preferred_element_type=F32) for i in range(2)
        ]
        canvas_grad = jnp.dot(picks[...], grads[:, wide], preferred_element_type=F32)
        made = []
        for i in range(2):
            parts = []
            for head in range(count):
                columns = slice(head * TASK_C, (head + 1) * TASK_C)
                output, dproject, gain_grad = head_chain(
                    projects[i][:, columns], canvas_grad[:, columns], gains[i][:, columns]
                )
                gain_grads[i][:, columns] = gain_grad
                parts.append((output, dproject))
            made.append(jnp.concatenate([part[0] for part in parts], axis=1))
            dproject = jnp.concatenate([part[1] for part in parts], axis=1)
            weight_grad = jnp.dot(
                turned[i][...], dproject, preferred_element_type=F32
            ).astype(BF16)
            if split:
                first = place.core == 0
                for head in range(count):
                    columns = slice(head * TASK_C, (head + 1) * TASK_C)
                    runs = weight_grad[:, columns].reshape(
                        C_MID // (2 * split), 2, split // 16, 16, TASK_C
                    )
                    ours = jnp.where(first, runs[:, 0], runs[:, 1])
                    others = jnp.where(first, runs[:, 1], runs[:, 0])
                    keeps[i][:, head] = ours.reshape(C_MID // 32, 16, TASK_C)
                    sends[i][:, head] = others.reshape(C_MID // 32, 16, TASK_C)
            else:
                keeps[i][:, wide] = weight_grad
            back = lax.dot_general(
                dproject,
                heads[i][:, wide],
                (((1,), (1,)), ((), ())),
                preferred_element_type=F32,
            )
            tap_grads[i][...] = jnp.where(step == 0, 0.0, tap_grads[i][...]) + back
        block[:, wide] = (made[0].astype(F32) + made[1].astype(F32)).astype(BF16)
        out[:, wide] = block[:, wide]
        start = jnp.where(place.big, (1 - own) * HALF, 0)
        send_out[:, wide] = block[pl.ds(aligned(start), HALF), wide]

    @pl.when(step < TASKS // 2)
    def _():
        some_heads(2)

    @pl.when(step == TASKS // 2)
    def _():
        some_heads(1)
        ride.work()
        ride.finish()


def run_heads(marks, facts, grad_own, grad_other, tops, heads, gains, after, steps):
    pair = 2 * TASK_C
    tile = lambda rows: pl.BlockSpec((rows, pair), lambda i: (0, i))
    whole = lambda shape: pl.BlockSpec(shape, lambda i: (0, 0))
    chains = [Chain(1, TASKS * C_MID) for _ in range(2)]
    split = chains[0].run(0) // TASKS
    if chains[0].block == 16 * TASKS:
        blocks = C_MID // 32
        grads = [jax.ShapeDtypeStruct((blocks, TASKS, 16, TASK_C), BF16)] * 4
        grad_specs = [pl.BlockSpec((blocks, 2, 16, TASK_C), lambda i: (0, i, 0, 0))] * 4
    else:
        split = None
        grads = [shape(C_MID, HEAD_OUT)] * 2
        grad_specs = [tile(C_MID)] * 2
    out, send_out, entered, *made = kernel_call(
        functools.partial(head_kernel, split),
        "heads",
        marks,
        [
            *facts,
            grad_own,
            grad_other,
            *tops,
            *heads,
            *[gain.reshape(1, HEAD_OUT) for gain in gains],
        ],
        [SMEM] * 2
        + [tile(HALF)] * 2
        + [whole((PIXELS, C_MID)), pl.BlockSpec((PIXELS, C_MID), lambda i: (3, 0))]
        + [tile(C_MID)] * 2
        + [tile(1)] * 2,
        [shape(PIXELS, HEAD_OUT), shape(HALF, HEAD_OUT), shape(*tops[1].shape)]
        + grads
        + [shape(1, HEAD_OUT, F32)] * 2
        + [shape(PIXELS, C_MID, F32)] * 2,
        [tile(PIXELS), tile(HALF), HBM]
        + grad_specs
        + [tile(1)] * 2
        + [whole((PIXELS, C_MID))] * 2,
        [buffer(PIXELS, PIXELS), buffer(PIXELS, pair), buffer(PIXELS, pair)]
        + [buffer(C_MID, PIXELS)] * 2,
        4 * PIXELS * HEAD_OUT * (3 * C_MID + PIXELS),
        after,
        steps,
        grid=(TASKS // 2 + 1,),
        aliases=[(5, 2)],
    )
    if split is None:
        parts, made = made[:2], made[2:]
        for chain, part in zip(chains, parts):
            blocks = part.reshape(-1, chain.block // TASKS, TASKS, TASK_C).swapaxes(1, 2)
            first_exchange(chain, 0, blocks.reshape(-1, TASK_C), None)
    else:
        keeps, sends, made = made[:2], made[2:4], made[4:]
        for chain, keep, send in zip(chains, keeps, sends):
            first_exchange(chain, 0, keep.reshape(-1, TASK_C), send.reshape(-1, TASK_C))
    gain_grads = [part.reshape(TASKS, TASK_C) for part in made[:2]]
    return out, send_out, entered, chains, gain_grads, made[2:]


def first_exchange(chain, name, keep, send):
    if send is None:
        run = chain.run(name)
        bit = own_bit(name)
        width = chain.width
        whole = keep.reshape(-1, 2, run, width)
        choose = lambda which: lax.dynamic_index_in_dim(whole, which, 1, keepdims=False)
        keep, send = choose(bit).reshape(-1, width), choose(1 - bit).reshape(-1, width)
    chain.remove(name, (keep, 0), (exchange(send, name), 0))


def merge_kernel(ride, marks, extents, largest, own, other, out, picks):
    step = pl.program_id(0)
    place = Place(marks, extents, largest)
    start = pl.multiple_of(place.own * HALF, HALF)

    @pl.when(step == 0)
    def _():
        ride.begin()
        half, quarter, _ = sources(place, start, HALF)
        picks[...] = select_matrix(half, quarter, HALF)

    @pl.when(step == 3)
    def _():
        ride.work()

    def add(coarse, fine):
        read = lax.dot_general(
            picks[...], coarse, (((0,), (0,)), ((), ())), preferred_element_type=F32
        )
        out[...] = (read + fine.astype(F32)).astype(BF16)

    @pl.when(place.big)
    def _():
        add(other[...], own[pl.ds(start, HALF)])

    @pl.when(jnp.logical_not(place.big))
    def _():
        add(own[0:HALF], other[...])

    @pl.when(step == TASKS - 1)
    def _():
        ride.finish()


def run_merge(marks, facts, own, other, after, steps):
    tile = lambda rows: pl.BlockSpec((rows, TASK_C), lambda i: (0, i))
    (out,) = kernel_call(
        merge_kernel,
        "merge",
        marks,
        [*facts, own, other],
        [SMEM] * 2 + [tile(PIXELS), tile(HALF)],
        [shape(HALF, HEAD_OUT)],
        [tile(HALF)],
        [buffer(HALF, HALF)],
        2 * HALF * HALF * HEAD_OUT,
        after,
        steps,
        grid=(TASKS,),
    )
    return out


class BackTask:
    def __init__(self, depth, weights, slope, grads):
        self.depth, self.ins = depth, [weights, slope, *grads]
        self.final = depth == 0
        self.rows = weights.shape[0]
        self.fan = self.rows // 9
        self.flops = 2 * PIXELS * weights.size

    def scratch(self):
        return [
            buffer(self.rows, C_MID),
            buffer(PIXELS, C_MID),
            buffer(PIXELS, C_MID, F32),
            buffer(PIXELS, C_MID, F32),
            pltpu.VMEM((2, PIXELS, WIDTH), BF16),
            buffer(PIXELS + 2 * SIDE, C_MID, F32),
            pltpu.VMEM((3, PIXELS + 2 * EDGE, C_MID), BF16),
            buffer(PIXELS, self.fan, F32),
            buffer(PIXELS, self.fan),
            pltpu.SemaphoreType.DMA((3,)),
            pltpu.SemaphoreType.DMA((3,)),
            pltpu.SemaphoreType.DMA((3,)),
        ]

    def bind(self, place, marks, ins, scratch, own, other, back, above):
        self.place, self.above, self.back = place, above, back
        weights_hbm, slope_hbm, *grads_hbm = ins
        weights, slope, grad, more, halves, pad, copies, total, made, sems, in_sems, out_sems = scratch
        self.weights, self.slope, self.grads = weights, slope, [grad, more][: len(grads_hbm)]
        self.pad, self.copies, self.total, self.halves = pad, copies, total, halves
        copy = pltpu.make_async_copy
        wide = lambda ref: ref.reshape(3, 3, self.fan, C_MID)
        self.loads = [
            copy(wide(weights_hbm).at[:, column], wide(weights).at[:, column], sems.at[column])
            for column in range(3)
        ]
        self.small = [copy(slope_hbm, slope, in_sems.at[0])]
        for i, (there, here) in enumerate(zip(grads_hbm, self.grads)):
            self.small.append(copy(there, here, in_sems.at[1 + i]))
        self.stores = [
            copy(halves.at[0], own, out_sems.at[0]),
            copy(halves.at[1], other, out_sems.at[1]),
        ]
        self.made = made
        if back is not None:
            self.stores.append(copy(made if self.final else total, back, out_sems.at[2]))

    def start(self):
        for one in self.small:
            one.start()
        self.loads[1].start()

    def start_rest(self):
        self.loads[0].start()
        self.loads[2].start()

    def prepare(self, head=False):
        clear_edges(self.copies, EDGE)
        for one in self.small:
            one.wait()
        if head:
            self.start_rest()
        else:
            for one in self.loads:
                one.wait()
        self.head = head
        parts = [self.above.total] if self.above is not None else []
        parts += self.grads
        grad = parts[0][...]
        for part in parts[1:]:
            grad = grad + part[...]
        grad = grad * self.slope[...].astype(F32)
        rounded = grad.astype(BF16)
        low, high = rounded[:, :WIDTH], rounded[:, WIDTH:]
        first = self.place.core == 0
        self.halves[0] = jnp.where(first, low, high)
        self.halves[1] = jnp.where(first, high, low)
        self.stores[0].start()
        self.stores[1].start()
        self.spread(grad, 1)

    def spread(self, values, tap):
        spread(values, self.pad, self.copies, EDGE, DILATIONS[self.depth], True, (tap,))

    def tap(self, turn):
        if turn in (1, 4):
            self.spread(None, 0 if turn == 1 else 2)
        column = (1, 0, 2)[turn // 3]
        tap = 3 * (turn % 3) + column
        begin = tap_start(EDGE, tap // 3, DILATIONS[self.depth], True)
        if turn % 3 == 0 and self.head:
            self.loads[column].wait()
        part = lax.dot_general(
            self.copies[tap % 3, begin : begin + PIXELS],
            self.weights[tap * self.fan : (tap + 1) * self.fan],
            (((1,), (1,)), ((), ())),
            preferred_element_type=F32,
        )
        if turn == 0:
            self.total[...] = part
        else:
            self.total[...] += part

    def end(self):
        if self.back is not None:
            if self.final:
                self.made[...] = (self.total[...] * pixel_mask(self.place)).astype(BF16)
            self.stores[2].start()

    def finish(self):
        for one in self.stores:
            one.wait()


class WeightTask:
    def __init__(self, depth, fan, firsts, mine, theirs, grad_mine, grad_theirs):
        self.depth, self.fan, self.firsts = depth, fan, firsts
        self.spots = [grad_mine[1], grad_theirs[1]]
        self.ins = [mine, theirs, grad_mine[0], grad_theirs[0]]
        self.rows = 9 * fan
        self.width = WIDTH // len(firsts)
        self.chains = [Chain(1, self.rows, self.width) for _ in firsts]
        splits = [chain.run(first) for chain, first in zip(self.chains, firsts)]
        self.splits = [None if split % 16 else split for split in splits]
        self.flops = 4 * PIXELS * self.rows * WIDTH

    def outs(self):
        made = []
        for split in self.splits:
            if split is None:
                made.append(shape(self.rows, self.width))
            else:
                made += [shape(self.rows // 2, self.width)] * 2
        return made

    def scratch(self):
        return (
            [
                pltpu.VMEM((2, PIXELS, WIDTH), BF16),
                buffer(PIXELS + 2 * SIDE, WIDTH, F32),
                buffer(PIXELS + 2 * SIDE, WIDTH, F32),
                pltpu.VMEM((3, 2 * PIXELS + 4 * EDGE, WIDTH), BF16),
                buffer(2 * PIXELS, self.fan),
                pltpu.SemaphoreType.DMA((4,)),
            ]
            + [buffer(self.rows, self.width)] * len(self.firsts)
            + [
                pltpu.SemaphoreType.DMA((1 if split is None else self.rows // split,))
                for split in self.splits
            ]
        )

    def bind(self, marks, ins, outs, scratch):
        mine, theirs, grad_mine, grad_theirs = ins
        grads, pad, pad_two, copies, both, in_sems, *rest = scratch
        self.grads, self.pads, self.copies, self.both = grads, (pad, pad_two), copies, both
        self.parts, out_sems = rest[: len(self.splits)], rest[len(self.splits) :]
        copy = pltpu.make_async_copy
        rows = pl.ds(self.depth * PIXELS, PIXELS)
        fan = pl.ds(0, self.fan)
        self.small = [
            copy(grad_mine.at[pl.ds(self.spots[0], PIXELS)], grads.at[0], in_sems.at[0]),
            copy(grad_theirs.at[pl.ds(self.spots[1], PIXELS)], grads.at[1], in_sems.at[1]),
        ]
        self.loads = [
            copy(mine.at[rows, fan], both.at[pl.ds(0, PIXELS)], in_sems.at[2]),
            copy(theirs.at[rows, fan], both.at[pl.ds(PIXELS, PIXELS)], in_sems.at[3]),
        ]
        self.stores = []
        outs = list(outs)
        for split, name, part, sems in zip(self.splits, self.firsts, self.parts, out_sems):
            if split is None:
                self.stores.append((copy(part, outs.pop(0), sems.at[0]), self.rows))
                continue
            bit = marks[mark(name)]
            keep, send = outs.pop(0), outs.pop(0)
            for run in range(self.rows // (2 * split)):
                there = pl.ds(run * split, split)
                for side, (array, which) in enumerate(((keep, bit), (send, 1 - bit))):
                    here = pl.ds(aligned((2 * run + which) * split), split)
                    one = copy(part.at[here], array.at[there], sems.at[2 * run + side])
                    self.stores.append((one, (2 * run + 2) * split))

    def start(self):
        for one in self.small:
            one.start()

    def start_rest(self):
        for one in self.loads:
            one.start()

    def prepare(self, head=False):
        if head:
            self.start_rest()
        second = 2 * EDGE + PIXELS + EDGE
        for place, base in enumerate((EDGE, second)):
            clear_edges(self.copies, base)
            self.small[place].wait()
            values = self.grads[place].astype(F32)
            spread(values, self.pads[place], self.copies, base, DILATIONS[self.depth], True)
        for one in self.loads:
            one.wait()

    def tap(self, tap):
        dilation = DILATIONS[self.depth]
        begin = tap_start(EDGE, tap // 3, dilation, True)
        later = tap_start(2 * EDGE + PIXELS + EDGE, tap // 3, dilation, True)
        copies = self.copies
        shifted = jnp.concatenate(
            [copies[tap % 3, begin : begin + PIXELS], copies[tap % 3, later : later + PIXELS]],
            axis=0,
        )
        product = lax.dot_general(
            self.both[...], shifted, (((0,), (0,)), ((), ())), preferred_element_type=F32
        ).astype(BF16)
        rows = slice(tap * self.fan, (tap + 1) * self.fan)
        for place, part in enumerate(self.parts):
            part[rows] = product[:, place * self.width : (place + 1) * self.width]
        for one, last in self.stores:
            if tap * self.fan < last <= (tap + 1) * self.fan:
                one.start()

    def end(self):
        pass

    def finish(self):
        for one, _ in self.stores:
            one.wait()

    def take(self, made):
        for chain, first, split in zip(self.chains, self.firsts, self.splits):
            keep = made.pop(0)
            first_exchange(chain, first, keep, None if split is None else made.pop(0))


def gradient_kernel(tasks, ride, marks, extents, largest, *rest):
    rest = list(rest)

    def take(count):
        taken = rest[:count]
        del rest[:count]
        return taken

    place = Place(marks, extents, largest)
    backs = [task for task in tasks if isinstance(task, BackTask)]
    middle = (len(tasks) - 1) // 2
    ins = [take(len(task.ins)) for task in tasks]
    own, other, back = take(3) if backs else (None, None, None)
    outs = [take(len(task.outs())) if isinstance(task, WeightTask) else None for task in tasks]
    above = None
    for task, task_ins, task_outs in zip(tasks, ins, outs):
        scratch = take(len(task.scratch()))
        if isinstance(task, WeightTask):
            task.bind(marks, task_ins, task_outs, scratch)
        else:
            rows = pl.ds(backs.index(task) * PIXELS, PIXELS)
            last = back if task is backs[-1] else None
            task.bind(place, marks, task_ins, scratch, own.at[rows], other.at[rows], last, above)
            above = task
    tasks[0].start()
    tasks[0].prepare(True)
    ride.begin()
    for number, task in enumerate(tasks):
        following = tasks[number + 1] if number + 1 < len(tasks) else None
        free = isinstance(following, WeightTask) or following is not None and following.above is None
        for tap in range(9):
            if tap == 1 and following is not None:
                following.start()
                following.start_rest()
            task.tap(tap)
            if tap == 4 and free:
                following.prepare()
            if tap == 5 and number == middle:
                ride.work()
        task.end()
        if following is not None and not free:
            following.prepare()
    for task in tasks:
        task.finish()
    ride.finish()


def run_gradients(marks, facts, tasks, after, steps):
    backs = [task for task in tasks if isinstance(task, BackTask)]
    weights = [task for task in tasks if isinstance(task, WeightTask)]
    outs = []
    if backs:
        rows = len(backs) * PIXELS
        last = backs[-1]
        outs += [shape(rows, WIDTH), shape(rows, WIDTH)]
        outs.append(shape(PIXELS, last.fan, BF16 if last.final else F32))
    for task in weights:
        outs += task.outs()
    made = kernel_call(
        functools.partial(gradient_kernel, tasks),
        "gradients",
        marks,
        [*facts, *[one for task in tasks for one in task.ins]],
        [SMEM] * 2 + [HBM] * sum(len(task.ins) for task in tasks),
        outs,
        [HBM] * len(outs),
        [one for task in tasks for one in task.scratch()],
        sum(task.flops for task in tasks),
        after,
        steps,
    )
    token = made[0]
    own = other = back = None
    if backs:
        own, other, back = made[:3]
        made = made[3:]
    for task in weights:
        task.take(made)
    return own, other, back, token


def kernel_rows(parts):
    rows = parts[0].rows()
    mine = [rows_of(chain.keep, rows) for chain in parts]
    other = [rows_of(chain.came, rows) for chain in parts]
    core = own_bit(0)
    pieces = [jnp.where(core == 0, a, b) for a, b in zip(mine, other)]
    pieces += [jnp.where(core == 0, b, a) for a, b in zip(mine, other)]
    return jnp.concatenate(pieces, axis=1).astype(F32).reshape(-1)


def head_rows(chain):
    rows = chain.rows()
    total = rows_of(chain.keep, rows).astype(F32) + rows_of(chain.came, rows).astype(F32)
    return total.reshape(TASKS, -1, TASK_C).swapaxes(0, 1).reshape(-1)


def on_device(
    features,
    extents,
    canvas_large,
    label_mask,
    kernel_one,
    kernel_two,
    kernel_three,
    kernel_four,
    kernel_five,
    kernel_six,
    affine_scale,
    affine_shift,
    head_lower,
    head_upper,
    gain_lower,
    gain_upper,
    merged_grad,
):
    kernels = (kernel_one, kernel_two, kernel_three, kernel_four, kernel_five, kernel_six)
    own = lax.axis_index("scale")
    marks = jnp.stack([own] + [own_bit(i) for i in range(bits())]).astype(jnp.int32)
    facts = (extents, canvas_large)
    far = list(range(2, bits()))

    grad_own = (merged_grad * label_mask[..., None].astype(BF16)).reshape(HALF, HEAD_OUT)
    grad_other = exchange(grad_own, "scale")

    entered, top, slopes = run_forward(
        marks,
        facts,
        features.reshape(PIXELS, -1),
        affine_scale,
        affine_shift,
        kernels,
        [grad_own],
    )
    halves = {}

    def backward(depth, *grads):
        return BackTask(depth, kernels[depth], slopes[depth], grads)

    def weight(depth, *firsts):
        fan = kernels[depth].shape[0] // 9
        return WeightTask(depth, fan, firsts, entered, partner, *halves.pop(depth))

    def gradients(after, steps, *tasks):
        own_halves, other, back, token = run_gradients(marks, facts, tasks, after, steps)
        depths = [task.depth for task in tasks if isinstance(task, BackTask)]
        if depths:
            came = exchange(other, 0)
            for place, depth in enumerate(depths):
                halves[depth] = ((own_halves, place * PIXELS), (came, place * PIXELS))
        return back, token

    z0 = 2 if far else 1
    summed_taps, taps_send, entered, (u, l), gain_grads, (back, back_lower) = run_heads(
        marks,
        facts,
        grad_own,
        grad_other,
        (top, entered),
        (head_upper, head_lower),
        (gain_upper, gain_lower),
        [],
        [],
    )
    gain_grads = gain_grads[::-1]
    partner = exchange(entered, 0)
    taps_other = exchange(taps_send, "scale")
    gains = jnp.concatenate(gain_grads)
    gains = jnp.pad(gains, ((0, 16 - 2 * TASKS), (0, 0)))
    high = gains.astype(BF16)
    gains = Totals(jnp.concatenate([high, (gains - high.astype(F32)).astype(BF16)]))
    gains.remove(0, gains.keep, (exchange(gains.keep[0], 0), 0))
    def some(name, *chains):
        return Step(name, *[chain for chain in chains if name in chain.names])

    def batch(after, *steps):
        def kernel(ride, marks_ref):
            ride.begin()
            ride.work()
            ride.finish()

        steps = [step for step in steps if step.chains]
        if not steps:
            return after
        kernel_call(kernel, "sums", marks, [], [], [], [], [], 1, [after], steps)
        return steps[0].chains[0].keep[0]

    z1 = far[1] if far[1:] else None
    ul = (u, l, gains)
    back, token = gradients([taps_send], [], backward(5, back), backward(4))
    t6, t5 = weight(5, 1), weight(4, z0)
    steps = [Step("scale", *ul)]
    back, token = gradients([token], steps, backward(3, back), backward(2, back_lower), t6, t5)
    (w6,), (w5,) = t6.chains, t5.chains
    t4, t3 = weight(3, 1), weight(2, z0)
    back, token = gradients([token, taps_other], [], backward(1, back), backward(0), t4, t3)
    (w4,), (w3,) = t4.chains, t3.chains
    t2, t1 = weight(1, "scale"), weight(0, 1)
    _, token = gradients([token], [some(z0, w6), some(z1, w5)], t2, t1)
    (w2,), (w1,) = t2.chains, t1.chains
    merged = run_merge(marks, facts, summed_taps, taps_other, [token], [])
    order = batch(merged, some(z0, w4), Step("scale", w3), some(1, *ul))
    order = batch(order, some(1, w2), some(z1, w6), Step("scale", w5), some(z0, w1))
    order = batch(order, some(z1, w4), some(1, w3), some(z0, *ul))
    order = batch(order, some(z0, w2), Step("scale", w6), some(1, w5), some(z1, w1))
    order = batch(order, Step("scale", w4), some(z1, w3), some(z1, *ul))
    for name in far[2:]:
        for chain in (u, l, gains, w6, w5, w4, w3, w1):
            Step(name, chain).go()
    order = batch(order, some(z1, w2), Step(0, w6, w5), Step("scale", w1))
    for name in far[2:]:
        Step(name, w2).go()
    order = batch(order, Step(0, w4, w3))
    Step(0, w2, w1).go()
    chains = [[w1], [w2], [w3], [w4], [w5], [w6]]
    share = HEAD_OUT // (lax.axis_size("img") * lax.axis_size("scale"))
    spot = lax.axis_index("img") * lax.axis_size("scale") + own
    added = gains.add(rows_of(gains.keep, gains.count), rows_of(gains.came, gains.count))
    added = added[0].astype(F32) + added[1].astype(F32)
    added = added[: 2 * TASKS].reshape(2, HEAD_OUT)
    gains = lax.dynamic_slice_in_dim(added, spot * share, share, 1)

    features_grad = back.reshape(features.shape)
    return (
        merged.reshape(merged_grad.shape),
        features_grad,
        *[kernel_rows(parts) for parts in chains],
        head_rows(l),
        head_rows(u),
        gains[0],
        gains[1],
    )


def solution(mesh):
    in_specs = (
        P("img", "scale", None, None, None),
        P("img", None),
        P("img"),
        P("img", "scale", None),
        P(),
        P(),
        P(),
        P(),
        P(),
        P(),
        P(),
        P(),
        P(),
        P(),
        P(),
        P(),
        P("img", "scale", None, None),
    )
    out_specs = (
        P("img", "scale", None, None),
        P("img", "scale", None, None, None),
        P(("img", "scale")),
        P(("img", "scale")),
        P(("img", "scale")),
        P(("img", "scale")),
        P(("img", "scale")),
        P(("img", "scale")),
        P(("img", "scale")),
        P(("img", "scale")),
        P(("img", "scale")),
        P(("img", "scale")),
    )
    return jax.shard_map(
        on_device, mesh=mesh, in_specs=in_specs, out_specs=out_specs, check_vma=False
    )
```

```python
import functools

import jax
import jax.numpy as jnp
from jax import lax
from jax.experimental import pallas as pl
from jax.experimental.pallas import tpu as pltpu
from jax.sharding import PartitionSpec as P

C_MID = 512
TASKS = 7
TASK_C = 256
HEAD_OUT = 1792
CANVAS = 24
PIXELS = CANVAS * CANVAS
HALF = PIXELS // 2
DILATIONS = (1, 1, 1, 2, 2, 2)
EDGE = 48
SIDE = 8
WIDTH = 256
MEGABYTES = 63
START_COL = CANVAS // 2 + 2

BF16 = jnp.bfloat16
F32 = jnp.float32

SMEM = pl.BlockSpec(memory_space=pltpu.SMEM)
HBM = pl.BlockSpec(memory_space=pltpu.HBM)
VMEM = pl.BlockSpec(memory_space=pltpu.VMEM)
ANY = pl.BlockSpec(memory_space=pl.ANY)


def shape(rows, width, kind=BF16):
    return jax.ShapeDtypeStruct((rows, width), kind)


def buffer(rows, width, kind=BF16):
    return pltpu.VMEM((rows, width), kind)


def aligned(index):
    return pl.multiple_of(index, 16)


def bits():
    return lax.axis_size("img").bit_length() - 1


def own_bit(name):
    if name == "scale":
        return lax.axis_index("scale")
    return (lax.axis_index("img") >> name) & 1


def mark(name):
    return 0 if name == "scale" else 1 + name


def exchange(array, name):
    if name == "scale":
        return lax.ppermute(array, "scale", [(0, 1), (1, 0)])
    count = lax.axis_size("img")
    return lax.ppermute(array, "img", [(i, i ^ (1 << name)) for i in range(count)])


class Chain:
    def __init__(self, copies, rows, width=WIDTH):
        self.width = width
        self.names = list(reversed(range(bits()))) + ["scale"]
        self.block = rows // (2 ** len(self.names))
        self.copies = copies
        self.doubled = False
        self.keep = self.came = None

    def rows(self):
        return self.copies * self.block * 2 ** len(self.names)

    def run(self, name):
        return self.block * 2 ** (len(self.names) - 1 - self.names.index(name))

    def whole(self, name):
        return name == "scale" and self.block % 16 == 8 and self.names[-1] == "scale"

    def remove(self, name, keep, came):
        if self.keep is not None and self.whole(name):
            self.block, self.doubled = 2 * self.block, True
        self.names.remove(name)
        self.keep, self.came = keep, came


def rows_of(piece, rows):
    array, first = piece
    return lax.slice_in_dim(array, first, first + rows, axis=0)


class Totals(Chain):
    def __init__(self, keep):
        self.names = list(reversed(range(bits()))) + ["scale"]
        self.width = keep.shape[1]
        self.count = keep.shape[0]
        self.keep = (keep, 0)

    def rows(self):
        return self.count

    def run(self, name):
        return self.count

    def whole(self, name):
        return True

    def remove(self, name, keep, came):
        self.names.remove(name)
        self.keep, self.came = keep, came

    def split(self, total):
        high = total.astype(BF16)
        return high, (total - high.astype(F32)).astype(BF16)

    def add(self, mine, theirs):
        half = self.count // 2
        total = mine[:half].astype(F32) + theirs[:half].astype(F32)
        return self.split(total + (mine[half:].astype(F32) + theirs[half:].astype(F32)))


class Step:
    def __init__(self, name, *chains):
        self.name, self.chains = name, chains
        self.width = WIDTH
        self.all = [chain.whole(name) for chain in chains]
        self.sizes = [
            (chain.rows(), chain.rows() if whole else chain.run(name))
            for chain, whole in zip(chains, self.all)
        ]
        self.fits = all(run % 16 == 0 for _, run in self.sizes)
        self.left = [
            rows if whole else rows // 2 for whole, (rows, _) in zip(self.all, self.sizes)
        ]
        self.total = sum(self.left)

    def plain(self):
        bit = own_bit(self.name)
        keeps, sends = [], []
        for chain, (rows, run) in zip(self.chains, self.sizes):
            if isinstance(chain, Totals):
                both = jnp.concatenate(
                    chain.add(rows_of(chain.keep, rows), rows_of(chain.came, rows))
                )
                keeps.append(both)
                sends.append(both)
                continue
            both = rows_of(chain.keep, rows).astype(F32) + rows_of(chain.came, rows).astype(F32)
            if chain.whole(self.name):
                keeps.append(both.astype(BF16))
                sends.append(both.astype(BF16))
                continue
            both = both.astype(BF16).reshape(rows // (2 * run), 2, run, self.width)
            choose = lambda which: lax.dynamic_index_in_dim(both, which, 1, keepdims=False)
            keeps.append(choose(bit).reshape(rows // 2, self.width))
            sends.append(choose(1 - bit).reshape(rows // 2, self.width))
        return keeps, jnp.concatenate(sends) if len(sends) > 1 else sends[0]

    def done(self, keeps, send):
        came, first = exchange(send, self.name), 0
        for chain, keep, left in zip(self.chains, keeps, self.left):
            chain.remove(self.name, (keep, 0), (came, first))
            first += left

    def go(self):
        self.done(*self.plain())

    def operands(self):
        return [part[0] for chain in self.chains for part in (chain.keep, chain.came)]

    def outs(self):
        return [shape(left, self.width) for left in [*self.left, self.total]]

    def scratch(self):
        made = [buffer(rows, self.width) for rows, _ in self.sizes for _ in range(2)]
        count = 2 * len(self.sizes)
        return made + [pltpu.SemaphoreType.DMA((count,)), pltpu.SemaphoreType.DMA((count,))]

    def bind(self, marks, ins, outs, scratch):
        bit = marks[mark(self.name)]
        in_sems, out_sems = scratch[-2], scratch[-1]
        loads, stores, sums = [], [], []
        sent = 0
        for place, (chain, left, (rows, run)) in enumerate(
            zip(self.chains, self.left, self.sizes)
        ):
            mine, theirs = scratch[2 * place], scratch[2 * place + 1]
            loads.append((ins[2 * place].at[pl.ds(chain.keep[1], rows)], mine))
            loads.append((ins[2 * place + 1].at[pl.ds(chain.came[1], rows)], theirs))
            there = outs[-1].at[pl.ds(sent, left)]
            sent += left
            if self.all[place]:
                sums.append((chain, mine, theirs))
                stores += [(mine, outs[place]), (mine, there)]
                continue
            pairs = rows // (2 * run)
            view = lambda ref, pairs=pairs, run=run: ref.reshape(pairs, 2, run, self.width)
            part = lambda ref, pairs=pairs, run=run: ref.reshape(pairs, run, self.width)
            sums.append((None, view(mine), view(theirs)))
            stores.append((view(mine).at[:, bit], part(outs[place])))
            stores.append((view(theirs).at[:, 1 - bit], part(there)))

        def load():
            return [pltpu.make_async_copy(*one, in_sems.at[i]) for i, one in enumerate(loads)]

        def store():
            return [pltpu.make_async_copy(*one, out_sems.at[i]) for i, one in enumerate(stores)]

        def begin():
            for one in load():
                one.start()

        def work():
            for one in load():
                one.wait()
            for chain, mine, theirs in sums:
                if chain is None:
                    mine[:, bit] = mine[:, bit] + theirs[:, bit]
                    theirs[:, 1 - bit] = mine[:, 1 - bit] + theirs[:, 1 - bit]
                elif not isinstance(chain, Totals):
                    mine[...] = mine[...] + theirs[...]
                else:
                    half = chain.count // 2
                    high, low = chain.add(mine[...], theirs[...])
                    mine[0:half] = high
                    mine[half:] = low
            for one in store():
                one.start()

        def finish():
            for one in store():
                one.wait()

        return begin, work, finish


class Ride:
    def __init__(self, parts):
        self.parts = parts

    def begin(self):
        for begin, _, _ in self.parts:
            begin()

    def work(self):
        for _, work, _ in self.parts:
            work()

    def finish(self):
        for _, _, finish in self.parts:
            finish()


def kernel_call(
    kernel, name, marks, ins, in_specs, outs, out_specs, scratch, flops, after, steps, grid=(), weight=0.3, aliases=(), megabytes=MEGABYTES
):
    after = list(after)
    steps = [step for step in steps if step.chains]
    riders = [step for step in steps if step.fits]
    for step in steps:
        if not step.fits:
            keeps, send = step.plain()
            step.done(keeps, send)
            after.append(send)
    ride_ins = [step.operands() for step in riders]
    ride_outs = [step.outs() for step in riders]
    ride_scratch = [step.scratch() for step in riders]
    flat = lambda lists: [one for part in lists for one in part]

    def body(*refs):
        refs = list(refs)

        def take(count):
            taken = refs[:count]
            del refs[:count]
            return taken

        take(len(after))
        (marks_ref,) = take(1)
        r_ins = [take(len(part)) for part in ride_ins]
        used = take(len(ins) + len(outs))
        r_outs = [take(len(part)) for part in ride_outs]
        own = take(len(scratch))
        r_scratch = [take(len(part)) for part in ride_scratch]
        ride = Ride(
            [
                step.bind(marks_ref, *refs3)
                for step, *refs3 in zip(riders, r_ins, r_outs, r_scratch)
            ]
        )
        kernel(ride, marks_ref, *used, *own)

    results = pl.pallas_call(
        body,
        grid=grid,
        out_shape=[*outs, *flat(ride_outs)],
        in_specs=[ANY] * len(after) + [SMEM] + [ANY] * len(flat(ride_ins)) + in_specs,
        out_specs=[*out_specs] + [ANY] * len(flat(ride_outs)),
        scratch_shapes=[*scratch, *flat(ride_scratch)],
        compiler_params=pltpu.CompilerParams(vmem_limit_bytes=megabytes << 20),
        cost_estimate=pl.CostEstimate(
            flops=int(weight * flops), bytes_accessed=1 << 20, transcendentals=0
        ),
        input_output_aliases={
            len(after) + 1 + len(flat(ride_ins)) + one: other for one, other in aliases
        },
        name=name,
    )(*after, marks, *flat(ride_ins), *ins)
    made, rest = list(results[: len(outs)]), list(results[len(outs) :])
    for step, part in zip(riders, ride_outs):
        *keeps, send = rest[: len(part)]
        del rest[: len(part)]
        step.done(keeps, send)
    return made


class Place:
    def __init__(self, marks, extents, largest):
        self.height, self.breadth = extents[0, 0], extents[0, 1]
        self.own, self.core = marks[0], marks[1]
        self.big = largest[0] == self.own


def scaled(place, extent, level):
    product = (place * (extent >> level)).astype(F32) + 0.5
    return jnp.floor(product / extent.astype(F32)).astype(jnp.int32)


def sources(place, offset, count):
    spot = lax.broadcasted_iota(jnp.int32, (1, count), 1) + offset
    row, col = spot // CANVAS, spot % CANVAS
    valid = (row < place.height) & (col < place.breadth)
    half = scaled(row, place.height, 1) * CANVAS + scaled(col, place.breadth, 1)
    quarter = scaled(row, place.height, 2) * CANVAS + START_COL + scaled(col, place.breadth, 2)
    return jnp.where(valid, half, -1), jnp.where(valid, quarter, -1), jnp.where(valid, spot, -1)


def select_matrix(first, second, length):
    spot = lax.broadcasted_iota(jnp.int32, (length, first.shape[1]), 0)
    return ((spot == first).astype(F32) + (spot == second).astype(F32)).astype(BF16)


def pixel_mask(place):
    spot = lax.broadcasted_iota(jnp.int32, (PIXELS, 1), 0)
    row, col = spot // CANVAS, spot % CANVAS
    height, breadth = place.height, place.breadth
    large = ((row < height) & (col < breadth)).astype(F32)
    half = ((row < height >> 1) & (col < breadth >> 1)).astype(F32)
    quarter = (
        (row < height >> 2) & (col >= START_COL) & (col < START_COL + (breadth >> 2))
    ).astype(F32)
    return jnp.where(place.big, large, jnp.maximum(half, quarter))


def spread(values, pad, copies, base, dilation, flip, taps=(0, 1, 2)):
    if values is not None:
        pad[SIDE : SIDE + PIXELS] = values
    col = lax.broadcasted_iota(jnp.int32, (PIXELS, 1), 0) % CANVAS
    for tap in taps:
        shift = (1 - tap if flip else tap - 1) * dilation
        moved = pad[SIDE + shift : SIDE + shift + PIXELS]
        if shift != 0:
            inside = (col + shift >= 0) & (col + shift < CANVAS)
            moved = jnp.where(inside, moved, 0.0)
        copies[tap, base : base + PIXELS] = moved.astype(BF16)


def clear_edges(copies, base):
    width = copies.shape[2]
    for tap in range(3):
        copies[tap, base - EDGE : base] = jnp.zeros((EDGE, width), BF16)
        copies[tap, base + PIXELS : base + PIXELS + EDGE] = jnp.zeros((EDGE, width), BF16)


def tap_start(base, row_tap, dilation, flip):
    return base + (1 - row_tap if flip else row_tap - 1) * dilation * CANVAS


def forward_kernel(
    ride,
    marks,
    extents,
    largest,
    features,
    scale_hbm,
    shift_hbm,
    w1,
    w2,
    w3,
    w4,
    w5,
    w6,
    entered,
    top,
    g1,
    g2,
    g3,
    g4,
    g5,
    g6,
    weights,
    first,
    scale,
    shift,
    pad_in,
    pad,
    copies_in,
    copies,
    total,
    made_e,
    made_g,
    sems,
    out_sems,
    small_sems,
):
    kernels = (w1, w2, w3, w4, w5, w6)
    slopes = (g1, g2, g3, g4, g5, g6)
    copy = pltpu.make_async_copy

    def load(layer):
        rows = kernels[layer].shape[0]
        return copy(kernels[layer], weights.at[layer % 2, pl.ds(0, rows)], sems.at[layer % 2])

    def store_e(layer):
        there = top if layer == 6 else entered.at[pl.ds(layer * PIXELS, PIXELS)]
        return copy(made_e.at[layer % 2], there, out_sems.at[0, layer % 2])

    def store_g(layer):
        return copy(made_g.at[layer % 2], slopes[layer], out_sems.at[1, layer % 2])

    small = [
        copy(features, first, small_sems.at[0]),
        copy(scale_hbm, scale, small_sems.at[1]),
        copy(shift_hbm, shift, small_sems.at[2]),
    ]
    for one in small:
        one.start()
    load(0).start()
    mask = pixel_mask(Place(marks, extents, largest))
    clear_edges(copies_in, EDGE)
    clear_edges(copies, EDGE)
    for one in small:
        one.wait()
    fan = features.shape[1]
    current = first[...].astype(F32) * mask
    made_e[0] = jnp.zeros_like(made_e[0])
    made_e[0, :, 0:fan] = current.astype(BF16)
    store_e(0).start()
    for layer in range(6):
        dilation = DILATIONS[layer]
        fan = kernels[layer].shape[0] // 9
        source = copies_in if layer == 0 else copies
        spread(current, pad_in if layer == 0 else pad, source, EDGE, dilation, False)
        load(layer).wait()
        if layer + 1 < 6:
            load(layer + 1).start()
        for row_tap in range(3):
            begin = tap_start(EDGE, row_tap, dilation, False)
            for col_tap in range(3):
                tap = 3 * row_tap + col_tap
                part = jnp.dot(
                    source[col_tap, begin : begin + PIXELS],
                    weights[layer % 2, tap * fan : (tap + 1) * fan],
                    preferred_element_type=F32,
                )
                if tap == 0:
                    total[...] = part
                else:
                    total[...] += part
        factor = scale[layer : layer + 1]
        h = total[...] * factor + shift[layer : layer + 1]
        root = 0.7978845608028654
        square = h * h
        t = jnp.tanh(h * (root + 0.044715 * root * square))
        rise = 0.5 + 0.5 * t
        current = h * rise
        slope = rise + (current - current * t) * (root + 0.134145 * root * square)
        if layer >= 2:
            store_g(layer - 2).wait()
        if layer >= 1:
            store_e(layer - 1).wait()
        made_g[layer % 2] = (slope * (factor * mask)).astype(BF16)
        current = mask * current
        made_e[(layer + 1) % 2] = current.astype(BF16)
        store_e(layer + 1).start()
        store_g(layer).start()
    for layer in (4, 5):
        store_e(layer + 1).wait()
        store_g(layer).wait()


def run_forward(marks, facts, features, scale, shift, kernels, after):
    fan = features.shape[1]
    rows = kernels[1].shape[0]
    entered, top, *slopes = kernel_call(
        forward_kernel,
        "trunk_forward",
        marks,
        [*facts, features, scale, shift, *kernels],
        [SMEM] * 2 + [HBM] * 9,
        [shape(6 * PIXELS, C_MID)] + [shape(PIXELS, C_MID)] * 7,
        [HBM] * 8,
        [
            pltpu.VMEM((2, rows, C_MID), BF16),
            buffer(PIXELS, fan),
            buffer(6, C_MID, F32),
            buffer(6, C_MID, F32),
            buffer(PIXELS + 2 * SIDE, fan, F32),
            buffer(PIXELS + 2 * SIDE, C_MID, F32),
            pltpu.VMEM((3, PIXELS + 2 * EDGE, fan), BF16),
            pltpu.VMEM((3, PIXELS + 2 * EDGE, C_MID), BF16),
            buffer(PIXELS, C_MID, F32),
            pltpu.VMEM((2, PIXELS, C_MID), BF16),
            pltpu.VMEM((2, PIXELS, C_MID), BF16),
            pltpu.SemaphoreType.DMA((2,)),
            pltpu.SemaphoreType.DMA((2, 2)),
            pltpu.SemaphoreType.DMA((3,)),
        ],
        sum(2 * PIXELS * k.size for k in kernels),
        after,
        [],
        weight=2.5,
    )
    return entered, top, slopes


def head_chain(project, canvas_grad, factor):
    inverse = lax.rsqrt(jnp.sum(project * project, axis=1, keepdims=True) + 1e-06)
    made = (project * inverse * factor).astype(BF16)
    scaled_grad = canvas_grad * inverse
    product = scaled_grad * project
    gain_grad = jnp.sum(product, axis=0, keepdims=True)
    inner = jnp.sum(product * factor, axis=1, keepdims=True) * (inverse * inverse)
    return made, (scaled_grad * factor - project * inner).astype(BF16), gain_grad


def head_kernel(split, ride, marks, extents, largest, labels, grad_own, grad_other, *rest):
    taps, heads, gains = rest[0:2], rest[2:4], rest[4]
    out, send_out, _, *rest = rest[5:]
    if split:
        keeps, sends, rest = rest[0:2], rest[2:4], rest[4:]
    else:
        keeps, sends, rest = rest[0:2], None, rest[2:]
    gain_grads, tap_grads, rest = rest[0:2], rest[2:4], rest[4:]
    picks, grads, block, *turned = rest
    step = pl.program_id(0)
    place = Place(marks, extents, largest)
    own = place.own

    @pl.when(step == 0)
    def _():
        ride.begin()
        half, quarter, same = sources(place, 0, PIXELS)
        labelled = labels[...] == 1
        first = jnp.where(place.big, same, half)
        second = jnp.where(place.big, -1, quarter)
        picks[...] = select_matrix(
            jnp.where(labelled, first, -1), jnp.where(labelled, second, -1), PIXELS
        )
        for i in range(2):
            turned[i][...] = taps[i][...].T

    def some_heads(count):
        wide = slice(0, count * TASK_C)
        grads[pl.ds(aligned(own * HALF), HALF), wide] = grad_own[:, wide]
        grads[pl.ds(aligned((1 - own) * HALF), HALF), wide] = grad_other[:, wide]
        projects = [
            jnp.dot(taps[i][...], heads[i][:, wide], preferred_element_type=F32) for i in range(2)
        ]
        canvas_grad = jnp.dot(picks[...], grads[:, wide], preferred_element_type=F32)
        made = []
        for i in range(2):
            parts = []
            for head in range(count):
                columns = slice(head * TASK_C, (head + 1) * TASK_C)
                output, dproject, gain_grad = head_chain(
                    projects[i][:, columns], canvas_grad[:, columns], gains[i : i + 1, columns]
                )
                gain_grads[i][:, columns] = gain_grad
                parts.append((output, dproject))
            made.append(jnp.concatenate([part[0] for part in parts], axis=1))
            dproject = jnp.concatenate([part[1] for part in parts], axis=1)
            weight_grad = jnp.dot(
                turned[i][...], dproject, preferred_element_type=F32
            ).astype(BF16)
            if split:
                first = place.core == 0
                for head in range(count):
                    columns = slice(head * TASK_C, (head + 1) * TASK_C)
                    runs = weight_grad[:, columns].reshape(
                        C_MID // (2 * split), 2, split // 16, 16, TASK_C
                    )
                    ours = jnp.where(first, runs[:, 0], runs[:, 1])
                    others = jnp.where(first, runs[:, 1], runs[:, 0])
                    keeps[i][:, head] = ours.reshape(C_MID // 32, 16, TASK_C)
                    sends[i][:, head] = others.reshape(C_MID // 32, 16, TASK_C)
            else:
                keeps[i][:, wide] = weight_grad
            back = lax.dot_general(
                dproject,
                heads[i][:, wide],
                (((1,), (1,)), ((), ())),
                preferred_element_type=F32,
            )
            tap_grads[i][...] = jnp.where(step == 0, 0.0, tap_grads[i][...]) + back
        block[:, wide] = (made[0].astype(F32) + made[1].astype(F32)).astype(BF16)
        out[:, wide] = block[:, wide]
        start = jnp.where(place.big, (1 - own) * HALF, 0)
        send_out[:, wide] = block[pl.ds(aligned(start), HALF), wide]

    @pl.when(step < TASKS // 2)
    def _():
        some_heads(2)

    @pl.when(step == TASKS // 2)
    def _():
        some_heads(1)
        ride.work()
        ride.finish()


def run_heads(marks, facts, labels, grad_own, grad_other, tops, heads, gains, after, steps):
    pair = 2 * TASK_C
    tile = lambda rows: pl.BlockSpec((rows, pair), lambda i: (0, i))
    whole = lambda shape: pl.BlockSpec(shape, lambda i: (0, 0))
    chains = [Chain(1, TASKS * C_MID) for _ in range(2)]
    split = chains[0].run(0) // TASKS
    if chains[0].block == 16 * TASKS:
        blocks = C_MID // 32
        grads = [jax.ShapeDtypeStruct((blocks, TASKS, 16, TASK_C), BF16)] * 4
        grad_specs = [pl.BlockSpec((blocks, 2, 16, TASK_C), lambda i: (0, i, 0, 0))] * 4
    else:
        split = None
        grads = [shape(C_MID, HEAD_OUT)] * 2
        grad_specs = [tile(C_MID)] * 2
    out, send_out, entered, *made = kernel_call(
        functools.partial(head_kernel, split),
        "heads",
        marks,
        [
            *facts,
            labels,
            grad_own,
            grad_other,
            *tops,
            *heads,
            jnp.stack(gains),
        ],
        [SMEM] * 2
        + [whole((1, PIXELS))]
        + [tile(HALF)] * 2
        + [whole((PIXELS, C_MID)), pl.BlockSpec((PIXELS, C_MID), lambda i: (3, 0))]
        + [tile(C_MID)] * 2
        + [tile(2)],
        [shape(PIXELS, HEAD_OUT), shape(HALF, HEAD_OUT), shape(*tops[1].shape)]
        + grads
        + [shape(1, HEAD_OUT, F32)] * 2
        + [shape(PIXELS, C_MID, F32)] * 2,
        [tile(PIXELS), tile(HALF), HBM]
        + grad_specs
        + [tile(1)] * 2
        + [whole((PIXELS, C_MID))] * 2,
        [buffer(PIXELS, PIXELS), buffer(PIXELS, pair), buffer(PIXELS, pair)]
        + [buffer(C_MID, PIXELS)] * 2,
        4 * PIXELS * HEAD_OUT * (3 * C_MID + PIXELS),
        after,
        steps,
        grid=(TASKS // 2 + 1,),
        aliases=[(6, 2)],
    )
    if split is None:
        parts, made = made[:2], made[2:]
        for chain, part in zip(chains, parts):
            blocks = part.reshape(-1, chain.block // TASKS, TASKS, TASK_C).swapaxes(1, 2)
            first_exchange(chain, 0, blocks.reshape(-1, TASK_C), None)
    else:
        keeps, sends, made = made[:2], made[2:4], made[4:]
        for chain, keep, send in zip(chains, keeps, sends):
            first_exchange(chain, 0, keep.reshape(-1, TASK_C), send.reshape(-1, TASK_C))
    gain_grads = [part.reshape(TASKS, TASK_C) for part in made[:2]]
    return out, send_out, entered, chains, gain_grads, made[2:]


def first_exchange(chain, name, keep, send):
    if send is None:
        run = chain.run(name)
        bit = own_bit(name)
        width = chain.width
        whole = keep.reshape(-1, 2, run, width)
        choose = lambda which: lax.dynamic_index_in_dim(whole, which, 1, keepdims=False)
        keep, send = choose(bit).reshape(-1, width), choose(1 - bit).reshape(-1, width)
    chain.remove(name, (keep, 0), (exchange(send, name), 0))


def merge_kernel(ride, marks, extents, largest, own, other, out, picks):
    step = pl.program_id(0)
    place = Place(marks, extents, largest)
    start = pl.multiple_of(place.own * HALF, HALF)

    @pl.when(step == 0)
    def _():
        ride.begin()
        half, quarter, _ = sources(place, start, HALF)
        picks[...] = select_matrix(half, quarter, HALF)

    @pl.when(step == 3)
    def _():
        ride.work()

    def add(coarse, fine):
        read = lax.dot_general(
            picks[...], coarse, (((0,), (0,)), ((), ())), preferred_element_type=F32
        )
        out[...] = (read + fine.astype(F32)).astype(BF16)

    @pl.when(place.big)
    def _():
        add(other[...], own[pl.ds(start, HALF)])

    @pl.when(jnp.logical_not(place.big))
    def _():
        add(own[0:HALF], other[...])

    @pl.when(step == TASKS - 1)
    def _():
        ride.finish()


def run_merge(marks, facts, own, other, after, steps):
    tile = lambda rows: pl.BlockSpec((rows, TASK_C), lambda i: (0, i))
    (out,) = kernel_call(
        merge_kernel,
        "merge",
        marks,
        [*facts, own, other],
        [SMEM] * 2 + [tile(PIXELS), tile(HALF)],
        [shape(HALF, HEAD_OUT)],
        [tile(HALF)],
        [buffer(HALF, HALF)],
        2 * HALF * HALF * HEAD_OUT,
        after,
        steps,
        grid=(TASKS,),
        weight=20,
    )
    return out


class BackTask:
    def __init__(self, depth, weights, slope, grads):
        self.depth, self.ins = depth, [weights, slope, *grads]
        self.final = depth == 0
        self.rows = weights.shape[0]
        self.fan = self.rows // 9
        self.flops = 2 * PIXELS * weights.size

    def scratch(self):
        return [
            buffer(self.rows, C_MID),
            buffer(PIXELS, C_MID),
            buffer(PIXELS, C_MID, F32),
            buffer(PIXELS, C_MID, F32),
            pltpu.VMEM((2, PIXELS, WIDTH), BF16),
            buffer(PIXELS + 2 * SIDE, C_MID, F32),
            pltpu.VMEM((3, PIXELS + 2 * EDGE, C_MID), BF16),
            buffer(PIXELS, self.fan, F32),
            buffer(PIXELS, self.fan),
            pltpu.SemaphoreType.DMA((3,)),
            pltpu.SemaphoreType.DMA((3,)),
            pltpu.SemaphoreType.DMA((3,)),
        ]

    def bind(self, place, marks, ins, scratch, own, other, back, above):
        self.place, self.above, self.back = place, above, back
        weights_hbm, slope_hbm, *grads_hbm = ins
        weights, slope, grad, more, halves, pad, copies, total, made, sems, in_sems, out_sems = scratch
        self.weights, self.slope, self.grads = weights, slope, [grad, more][: len(grads_hbm)]
        self.pad, self.copies, self.total, self.halves = pad, copies, total, halves
        copy = pltpu.make_async_copy
        wide = lambda ref: ref.reshape(3, 3, self.fan, C_MID)
        self.loads = [
            copy(wide(weights_hbm).at[:, column], wide(weights).at[:, column], sems.at[column])
            for column in range(3)
        ]
        self.small = [copy(slope_hbm, slope, in_sems.at[0])]
        for i, (there, here) in enumerate(zip(grads_hbm, self.grads)):
            self.small.append(copy(there, here, in_sems.at[1 + i]))
        self.stores = [
            copy(halves.at[0], own, out_sems.at[0]),
            copy(halves.at[1], other, out_sems.at[1]),
        ]
        self.made = made
        if back is not None:
            self.stores.append(copy(made if self.final else total, back, out_sems.at[2]))

    def start(self):
        for one in self.small:
            one.start()
        self.loads[1].start()

    def start_rest(self):
        self.loads[0].start()
        self.loads[2].start()

    def prepare(self, head=False):
        clear_edges(self.copies, EDGE)
        for one in self.small:
            one.wait()
        if head:
            self.start_rest()
        else:
            for one in self.loads:
                one.wait()
        self.head = head
        parts = [self.above.total] if self.above is not None else []
        parts += self.grads
        grad = parts[0][...]
        for part in parts[1:]:
            grad = grad + part[...]
        grad = grad * self.slope[...].astype(F32)
        rounded = grad.astype(BF16)
        low, high = rounded[:, :WIDTH], rounded[:, WIDTH:]
        first = self.place.core == 0
        self.halves[0] = jnp.where(first, low, high)
        self.halves[1] = jnp.where(first, high, low)
        self.stores[0].start()
        self.stores[1].start()
        self.spread(grad, 1)

    def spread(self, values, tap):
        spread(values, self.pad, self.copies, EDGE, DILATIONS[self.depth], True, (tap,))

    def tap(self, turn):
        if turn in (1, 4):
            self.spread(None, 0 if turn == 1 else 2)
        column = (1, 0, 2)[turn // 3]
        tap = 3 * (turn % 3) + column
        begin = tap_start(EDGE, tap // 3, DILATIONS[self.depth], True)
        if turn % 3 == 0 and self.head:
            self.loads[column].wait()
        part = lax.dot_general(
            self.copies[tap % 3, begin : begin + PIXELS],
            self.weights[tap * self.fan : (tap + 1) * self.fan],
            (((1,), (1,)), ((), ())),
            preferred_element_type=F32,
        )
        if turn == 0:
            self.total[...] = part
        else:
            self.total[...] += part

    def end(self):
        if self.back is not None:
            if self.final:
                self.made[...] = (self.total[...] * pixel_mask(self.place)).astype(BF16)
            self.stores[2].start()

    def finish(self):
        for one in self.stores:
            one.wait()


class WeightTask:
    def __init__(self, depth, fan, firsts, mine, theirs, grad_mine, grad_theirs):
        self.depth, self.fan, self.firsts = depth, fan, firsts
        self.spots = [grad_mine[1], grad_theirs[1]]
        self.ins = [mine, theirs, grad_mine[0], grad_theirs[0]]
        self.rows = 9 * fan
        self.width = WIDTH // len(firsts)
        self.chains = [Chain(1, self.rows, self.width) for _ in firsts]
        splits = [chain.run(first) for chain, first in zip(self.chains, firsts)]
        self.splits = [None if split % 16 else split for split in splits]
        self.flops = 4 * PIXELS * self.rows * WIDTH

    def outs(self):
        made = []
        for split in self.splits:
            if split is None:
                made.append(shape(self.rows, self.width))
            else:
                made += [shape(self.rows // 2, self.width)] * 2
        return made

    def scratch(self):
        return (
            [
                pltpu.VMEM((2, PIXELS, WIDTH), BF16),
                buffer(PIXELS + 2 * SIDE, WIDTH, F32),
                buffer(PIXELS + 2 * SIDE, WIDTH, F32),
                pltpu.VMEM((3, 2 * PIXELS + 4 * EDGE, WIDTH), BF16),
                buffer(2 * PIXELS, self.fan),
                pltpu.SemaphoreType.DMA((4,)),
            ]
            + [buffer(self.rows, self.width)] * len(self.firsts)
            + [
                pltpu.SemaphoreType.DMA((1 if split is None else self.rows // split,))
                for split in self.splits
            ]
        )

    def bind(self, marks, ins, outs, scratch):
        mine, theirs, grad_mine, grad_theirs = ins
        grads, pad, pad_two, copies, both, in_sems, *rest = scratch
        self.grads, self.pads, self.copies, self.both = grads, (pad, pad_two), copies, both
        self.parts, out_sems = rest[: len(self.splits)], rest[len(self.splits) :]
        copy = pltpu.make_async_copy
        rows = pl.ds(self.depth * PIXELS, PIXELS)
        fan = pl.ds(0, self.fan)
        self.small = [
            copy(grad_mine.at[pl.ds(self.spots[0], PIXELS)], grads.at[0], in_sems.at[0]),
            copy(grad_theirs.at[pl.ds(self.spots[1], PIXELS)], grads.at[1], in_sems.at[1]),
        ]
        self.loads = [
            copy(mine.at[rows, fan], both.at[pl.ds(0, PIXELS)], in_sems.at[2]),
            copy(theirs.at[rows, fan], both.at[pl.ds(PIXELS, PIXELS)], in_sems.at[3]),
        ]
        self.stores = []
        outs = list(outs)
        for split, name, part, sems in zip(self.splits, self.firsts, self.parts, out_sems):
            if split is None:
                self.stores.append((copy(part, outs.pop(0), sems.at[0]), self.rows))
                continue
            bit = marks[mark(name)]
            keep, send = outs.pop(0), outs.pop(0)
            for run in range(self.rows // (2 * split)):
                there = pl.ds(run * split, split)
                for side, (array, which) in enumerate(((keep, bit), (send, 1 - bit))):
                    here = pl.ds(aligned((2 * run + which) * split), split)
                    one = copy(part.at[here], array.at[there], sems.at[2 * run + side])
                    self.stores.append((one, (2 * run + 2) * split))

    def start(self):
        for one in self.small:
            one.start()

    def start_rest(self):
        for one in self.loads:
            one.start()

    def prepare(self, head=False):
        if head:
            self.start_rest()
        second = 2 * EDGE + PIXELS + EDGE
        for place, base in enumerate((EDGE, second)):
            clear_edges(self.copies, base)
            self.small[place].wait()
            values = self.grads[place].astype(F32)
            spread(values, self.pads[place], self.copies, base, DILATIONS[self.depth], True)
        for one in self.loads:
            one.wait()

    def tap(self, tap):
        dilation = DILATIONS[self.depth]
        begin = tap_start(EDGE, tap // 3, dilation, True)
        later = tap_start(2 * EDGE + PIXELS + EDGE, tap // 3, dilation, True)
        copies = self.copies
        shifted = jnp.concatenate(
            [copies[tap % 3, begin : begin + PIXELS], copies[tap % 3, later : later + PIXELS]],
            axis=0,
        )
        product = lax.dot_general(
            self.both[...], shifted, (((0,), (0,)), ((), ())), preferred_element_type=F32
        ).astype(BF16)
        rows = slice(tap * self.fan, (tap + 1) * self.fan)
        for place, part in enumerate(self.parts):
            part[rows] = product[:, place * self.width : (place + 1) * self.width]
        for one, last in self.stores:
            if tap * self.fan < last <= (tap + 1) * self.fan:
                one.start()

    def end(self):
        pass

    def finish(self):
        for one, _ in self.stores:
            one.wait()

    def take(self, made):
        for chain, first, split in zip(self.chains, self.firsts, self.splits):
            keep = made.pop(0)
            first_exchange(chain, first, keep, None if split is None else made.pop(0))


def gradient_kernel(tasks, ride, marks, extents, largest, *rest):
    rest = list(rest)

    def take(count):
        taken = rest[:count]
        del rest[:count]
        return taken

    place = Place(marks, extents, largest)
    backs = [task for task in tasks if isinstance(task, BackTask)]
    middle = (len(tasks) - 1) // 2
    ins = [take(len(task.ins)) for task in tasks]
    own, other, back = take(3) if backs else (None, None, None)
    outs = [take(len(task.outs())) if isinstance(task, WeightTask) else None for task in tasks]
    above = None
    for task, task_ins, task_outs in zip(tasks, ins, outs):
        scratch = take(len(task.scratch()))
        if isinstance(task, WeightTask):
            task.bind(marks, task_ins, task_outs, scratch)
        else:
            rows = pl.ds(backs.index(task) * PIXELS, PIXELS)
            last = back if task is backs[-1] else None
            task.bind(place, marks, task_ins, scratch, own.at[rows], other.at[rows], last, above)
            above = task
    tasks[0].start()
    tasks[0].prepare(True)
    ride.begin()
    for number, task in enumerate(tasks):
        following = tasks[number + 1] if number + 1 < len(tasks) else None
        free = isinstance(following, WeightTask) or following is not None and following.above is None
        for tap in range(9):
            if tap == 1 and following is not None:
                following.start()
                following.start_rest()
            task.tap(tap)
            if tap == 4 and free:
                following.prepare()
            if tap == 5 and number == middle:
                ride.work()
        task.end()
        if following is not None and not free:
            following.prepare()
    for task in tasks:
        task.finish()
    ride.finish()


def run_gradients(marks, facts, tasks, after, steps):
    backs = [task for task in tasks if isinstance(task, BackTask)]
    weights = [task for task in tasks if isinstance(task, WeightTask)]
    outs = []
    if backs:
        rows = len(backs) * PIXELS
        last = backs[-1]
        outs += [shape(rows, WIDTH), shape(rows, WIDTH)]
        outs.append(shape(PIXELS, last.fan, BF16 if last.final else F32))
    for task in weights:
        outs += task.outs()
    made = kernel_call(
        functools.partial(gradient_kernel, tasks),
        "gradients",
        marks,
        [*facts, *[one for task in tasks for one in task.ins]],
        [SMEM] * 2 + [HBM] * sum(len(task.ins) for task in tasks),
        outs,
        [HBM] * len(outs),
        [one for task in tasks for one in task.scratch()],
        sum(task.flops for task in tasks),
        after,
        steps,
    )
    token = made[0]
    own = other = back = None
    if backs:
        own, other, back = made[:3]
        made = made[3:]
    for task in weights:
        task.take(made)
    return own, other, back, token


def joined(mine, other):
    core = own_bit(0)
    left, right = jnp.where(core == 0, mine, other), jnp.where(core == 0, other, mine)
    return jnp.concatenate([left, right], axis=1).reshape(-1)


def stacked(total):
    return total.reshape(TASKS, -1, TASK_C).swapaxes(0, 1).reshape(-1)


def final_kernel(layout, marks, *refs):
    count = len(layout)
    first = marks[1] == 0
    for (rows, whole, doubled, spot, other_spot), mine, other, out in zip(
        layout, refs[:count], refs[count : 2 * count], refs[2 * count :]
    ):
        mine = mine[spot : spot + rows].astype(F32)
        other = other[other_spot : other_spot + rows].astype(F32)
        if doubled:
            rows = rows // 2
            lower = marks[0] == 0
            mine = jnp.where(lower, mine[:rows], mine[rows:])
            other = jnp.where(lower, other[:rows], other[rows:])
        if whole:
            left, right = jnp.where(first, mine, other), jnp.where(first, other, mine)
            for part in range(4):
                half = left if part < 2 else right
                columns = slice(part % 2 * 128, part % 2 * 128 + 128)
                out[pl.ds(part, rows, stride=4)] = half[:, columns]
        else:
            total, block = mine + other, rows // TASKS
            for head in range(TASKS):
                for part in range(2):
                    out[pl.ds(2 * head + part, block, stride=2 * TASKS)] = total[
                        head * block : (head + 1) * block, part * 128 : part * 128 + 128
                    ]


def final_rows(marks, kernels, heads=()):
    chains = [*kernels, *heads]
    if any(chain.block % 8 for chain in chains):
        made = []
        for chain in chains:
            rows = chain.rows()
            mine = rows_of(chain.keep, rows).astype(F32)
            other = rows_of(chain.came, rows).astype(F32)
            made.append(joined(mine, other) if chain in kernels else stacked(mine + other))
        return made
    layout = [
        (chain.rows(), place < len(kernels), chain.doubled, chain.keep[1], chain.came[1])
        for place, chain in enumerate(chains)
    ]
    made = pl.pallas_call(
        functools.partial(final_kernel, layout),
        out_shape=[
            shape(rows * (4 if whole else 2) // (2 if doubled else 1), 128, F32)
            for rows, whole, doubled, _, _ in layout
        ],
        in_specs=[SMEM] + [VMEM] * (2 * len(chains)),
        out_specs=[VMEM] * len(chains),
        compiler_params=pltpu.CompilerParams(vmem_limit_bytes=24 << 20),
        name="final_rows",
    )(marks, *[chain.keep[0] for chain in chains], *[chain.came[0] for chain in chains])
    return [one.reshape(-1) for one in made]


def on_device(
    features,
    extents,
    canvas_large,
    label_mask,
    kernel_one,
    kernel_two,
    kernel_three,
    kernel_four,
    kernel_five,
    kernel_six,
    affine_scale,
    affine_shift,
    head_lower,
    head_upper,
    gain_lower,
    gain_upper,
    merged_grad,
):
    kernels = (kernel_one, kernel_two, kernel_three, kernel_four, kernel_five, kernel_six)
    own = lax.axis_index("scale")
    marks = jnp.stack([own] + [own_bit(i) for i in range(bits())]).astype(jnp.int32)
    facts = (extents, canvas_large)
    far = list(range(2, bits()))

    grad_own = merged_grad.reshape(HALF, HEAD_OUT)
    grad_other = exchange(grad_own, "scale")
    labels = label_mask.reshape(1, HALF)
    labels_other = exchange(labels, "scale")
    labels = jnp.where(
        own == 0,
        jnp.concatenate([labels, labels_other], axis=1),
        jnp.concatenate([labels_other, labels], axis=1),
    )

    entered, top, slopes = run_forward(
        marks,
        facts,
        features.reshape(PIXELS, -1),
        affine_scale,
        affine_shift,
        kernels,
        [],
    )
    halves = {}

    def backward(depth, *grads):
        return BackTask(depth, kernels[depth], slopes[depth], grads)

    def weight(depth, *firsts):
        fan = kernels[depth].shape[0] // 9
        return WeightTask(depth, fan, firsts, entered, partner, *halves.pop(depth))

    def gradients(after, steps, *tasks):
        own_halves, other, back, token = run_gradients(marks, facts, tasks, after, steps)
        depths = [task.depth for task in tasks if isinstance(task, BackTask)]
        if depths:
            came = exchange(other, 0)
            for place, depth in enumerate(depths):
                halves[depth] = ((own_halves, place * PIXELS), (came, place * PIXELS))
        return back, token

    z0 = 2 if far else 1
    summed_taps, taps_send, entered, (u, l), gain_grads, (back, back_lower) = run_heads(
        marks,
        facts,
        labels,
        grad_own,
        grad_other,
        (top, entered),
        (head_upper, head_lower),
        (gain_upper, gain_lower),
        [],
        [],
    )
    gain_grads = gain_grads[::-1]
    partner = exchange(entered, 0)
    taps_other = exchange(taps_send, "scale")
    gains = jnp.concatenate(gain_grads)
    gains = jnp.pad(gains, ((0, 16 - 2 * TASKS), (0, 0)))
    high = gains.astype(BF16)
    gains = Totals(jnp.concatenate([high, (gains - high.astype(F32)).astype(BF16)]))
    gains.remove(0, gains.keep, (exchange(gains.keep[0], 0), 0))
    def some(name, *chains):
        return Step(name, *[chain for chain in chains if name in chain.names])

    def batch(after, *steps):
        def kernel(ride, marks_ref):
            ride.begin()
            ride.work()
            ride.finish()

        steps = [step for step in steps if step.chains]
        if not steps:
            return after
        kernel_call(kernel, "sums", marks, [], [], [], [], [], 1, [after], steps)
        return steps[0].chains[0].keep[0]

    z1 = far[1] if far[1:] else None
    ul = (u, l)
    back, token = gradients([taps_send], [], backward(5, back), backward(4))
    t6, t5 = weight(5, 1), weight(4, z0)
    back, token = gradients([token], [], backward(3, back), backward(2, back_lower), t6, t5)
    (w6,), (w5,) = t6.chains, t5.chains
    t4, t3 = weight(3, 1), weight(2, z0)
    steps = [Step("scale", *ul)]
    back, token = gradients([token, taps_other], steps, backward(1, back), backward(0), t4, t3)
    (w4,), (w3,) = t4.chains, t3.chains
    t2, t1 = weight(1, "scale"), weight(0, 1)
    _, token = gradients([token], [some(z0, w6), some(z1, w5)], t2, t1)
    (w2,), (w1,) = t2.chains, t1.chains
    merged = run_merge(marks, facts, summed_taps, taps_other, [token], [])
    order = batch(merged, some(z0, w4), Step("scale", w3), some(1, *ul))
    order = batch(order, some(1, w2), some(z1, w6), Step("scale", w5, gains), some(z0, w1))
    order = batch(order, some(z1, w4), some(1, w3), some(z0, *ul))
    order = batch(order, some(z0, w2, gains), Step("scale", w6), some(1, w5), some(z1, w1))
    order = batch(order, Step("scale", w4), some(z1, w3), some(z1, *ul), some(1, gains))
    for name in far[2:]:
        for chain in (u, l, w6, w5, w4, w3, w1):
            Step(name, chain).go()
    order = batch(order, some(z1, w2, gains), Step(0, w6, w5), Step("scale", w1))
    for name in far[2:]:
        Step(name, w2).go()
        Step(name, gains).go()
    order = batch(order, Step(0, w4, w3))
    Step(0, w2, w1).go()
    g6, g5, gu, gl = final_rows(marks, [w6, w5], [u, l])
    g4, g3 = final_rows(marks, [w4, w3])
    g2, g1 = final_rows(marks, [w2, w1])

    share = HEAD_OUT // (lax.axis_size("img") * lax.axis_size("scale"))
    spot = lax.axis_index("img") * lax.axis_size("scale") + own
    added = gains.add(rows_of(gains.keep, gains.count), rows_of(gains.came, gains.count))
    added = added[0].astype(F32) + added[1].astype(F32)
    added = added[: 2 * TASKS].reshape(2, HEAD_OUT)
    gains = lax.dynamic_slice_in_dim(added, spot * share, share, 1)

    features_grad = back.reshape(features.shape)
    return (
        merged.reshape(merged_grad.shape),
        features_grad,
        *[g1, g2, g3, g4, g5, g6],
        gl,
        gu,
        gains[0],
        gains[1],
    )


def solution(mesh):
    in_specs = (
        P("img", "scale", None, None, None),
        P("img", None),
        P("img"),
        P("img", "scale", None),
        P(),
        P(),
        P(),
        P(),
        P(),
        P(),
        P(),
        P(),
        P(),
        P(),
        P(),
        P(),
        P("img", "scale", None, None),
    )
    out_specs = (
        P("img", "scale", None, None),
        P("img", "scale", None, None, None),
        P(("img", "scale")),
        P(("img", "scale")),
        P(("img", "scale")),
        P(("img", "scale")),
        P(("img", "scale")),
        P(("img", "scale")),
        P(("img", "scale")),
        P(("img", "scale")),
        P(("img", "scale")),
        P(("img", "scale")),
    )
    return jax.shard_map(
        on_device, mesh=mesh, in_specs=in_specs, out_specs=out_specs, check_vma=False
    )
```

```python
import functools

import jax
import jax.numpy as jnp
from jax import lax
from jax.experimental import pallas as pl
from jax.experimental.pallas import tpu as pltpu
from jax.sharding import PartitionSpec as P

C_MID = 512
TASKS = 7
TASK_C = 256
HEAD_OUT = 1792
CANVAS = 24
PIXELS = CANVAS * CANVAS
HALF = PIXELS // 2
DILATIONS = (1, 1, 1, 2, 2, 2)
EDGE = 48
SIDE = 8
WIDTH = 256
MEGABYTES = 63
START_COL = CANVAS // 2 + 2

BF16 = jnp.bfloat16
F32 = jnp.float32

SMEM = pl.BlockSpec(memory_space=pltpu.SMEM)
HBM = pl.BlockSpec(memory_space=pltpu.HBM)
VMEM = pl.BlockSpec(memory_space=pltpu.VMEM)
ANY = pl.BlockSpec(memory_space=pl.ANY)


def shape(rows, width, kind=BF16):
    return jax.ShapeDtypeStruct((rows, width), kind)


def buffer(rows, width, kind=BF16):
    return pltpu.VMEM((rows, width), kind)


def aligned(index):
    return pl.multiple_of(index, 16)


def bits():
    return lax.axis_size("img").bit_length() - 1


def own_bit(name):
    if name == "scale":
        return lax.axis_index("scale")
    return (lax.axis_index("img") >> name) & 1


def mark(name):
    return 0 if name == "scale" else 1 + name


def exchange(array, name):
    if name == "scale":
        return lax.ppermute(array, "scale", [(0, 1), (1, 0)])
    count = lax.axis_size("img")
    return lax.ppermute(array, "img", [(i, i ^ (1 << name)) for i in range(count)])


class Chain:
    def __init__(self, copies, rows, width=WIDTH):
        self.width = width
        self.names = list(reversed(range(bits()))) + ["scale"]
        self.block = rows // (2 ** len(self.names))
        self.copies = copies
        self.doubled = False
        self.keep = self.came = None

    def rows(self):
        return self.copies * self.block * 2 ** len(self.names)

    def run(self, name):
        return self.block * 2 ** (len(self.names) - 1 - self.names.index(name))

    def whole(self, name):
        return name == "scale" and self.block % 16 == 8 and self.names[-1] == "scale"

    def remove(self, name, keep, came):
        if self.keep is not None and self.whole(name):
            self.block, self.doubled = 2 * self.block, True
        self.names.remove(name)
        self.keep, self.came = keep, came


def rows_of(piece, rows):
    array, first = piece
    return lax.slice_in_dim(array, first, first + rows, axis=0)


class Totals(Chain):
    def __init__(self, keep):
        self.names = list(reversed(range(bits()))) + ["scale"]
        self.width = keep.shape[1]
        self.count = keep.shape[0]
        self.keep = (keep, 0)

    def rows(self):
        return self.count

    def run(self, name):
        return self.count

    def whole(self, name):
        return True

    def remove(self, name, keep, came):
        self.names.remove(name)
        self.keep, self.came = keep, came

    def split(self, total):
        high = total.astype(BF16)
        return high, (total - high.astype(F32)).astype(BF16)

    def add(self, mine, theirs):
        half = self.count // 2
        total = mine[:half].astype(F32) + theirs[:half].astype(F32)
        return self.split(total + (mine[half:].astype(F32) + theirs[half:].astype(F32)))


class Step:
    def __init__(self, name, *chains):
        self.name, self.chains = name, chains
        self.width = WIDTH
        self.all = [chain.whole(name) for chain in chains]
        self.sizes = [
            (chain.rows(), chain.rows() if whole else chain.run(name))
            for chain, whole in zip(chains, self.all)
        ]
        self.fits = all(run % 16 == 0 for _, run in self.sizes)
        self.left = [
            rows if whole else rows // 2 for whole, (rows, _) in zip(self.all, self.sizes)
        ]
        self.total = sum(self.left)

    def plain(self):
        bit = own_bit(self.name)
        keeps, sends = [], []
        for chain, (rows, run) in zip(self.chains, self.sizes):
            if isinstance(chain, Totals):
                both = jnp.concatenate(
                    chain.add(rows_of(chain.keep, rows), rows_of(chain.came, rows))
                )
                keeps.append(both)
                sends.append(both)
                continue
            both = rows_of(chain.keep, rows).astype(F32) + rows_of(chain.came, rows).astype(F32)
            if chain.whole(self.name):
                keeps.append(both.astype(BF16))
                sends.append(both.astype(BF16))
                continue
            both = both.astype(BF16).reshape(rows // (2 * run), 2, run, self.width)
            choose = lambda which: lax.dynamic_index_in_dim(both, which, 1, keepdims=False)
            keeps.append(choose(bit).reshape(rows // 2, self.width))
            sends.append(choose(1 - bit).reshape(rows // 2, self.width))
        return keeps, jnp.concatenate(sends) if len(sends) > 1 else sends[0]

    def done(self, keeps, send):
        came, first = exchange(send, self.name), 0
        for chain, keep, left in zip(self.chains, keeps, self.left):
            chain.remove(self.name, (keep, 0), (came, first))
            first += left

    def go(self):
        self.done(*self.plain())

    def operands(self):
        return [part[0] for chain in self.chains for part in (chain.keep, chain.came)]

    def outs(self):
        return [shape(left, self.width) for left in [*self.left, self.total]]

    def scratch(self):
        made = [buffer(rows, self.width) for rows, _ in self.sizes for _ in range(2)]
        count = 2 * len(self.sizes)
        return made + [pltpu.SemaphoreType.DMA((count,)), pltpu.SemaphoreType.DMA((count,))]

    def bind(self, marks, ins, outs, scratch):
        bit = marks[mark(self.name)]
        in_sems, out_sems = scratch[-2], scratch[-1]
        loads, stores, sums = [], [], []
        sent = 0
        for place, (chain, left, (rows, run)) in enumerate(
            zip(self.chains, self.left, self.sizes)
        ):
            mine, theirs = scratch[2 * place], scratch[2 * place + 1]
            loads.append((ins[2 * place].at[pl.ds(chain.keep[1], rows)], mine))
            loads.append((ins[2 * place + 1].at[pl.ds(chain.came[1], rows)], theirs))
            there = outs[-1].at[pl.ds(sent, left)]
            sent += left
            if self.all[place]:
                sums.append((chain, mine, theirs))
                stores += [(mine, outs[place]), (mine, there)]
                continue
            pairs = rows // (2 * run)
            view = lambda ref, pairs=pairs, run=run: ref.reshape(pairs, 2, run, self.width)
            part = lambda ref, pairs=pairs, run=run: ref.reshape(pairs, run, self.width)
            sums.append((None, view(mine), view(theirs)))
            stores.append((view(mine).at[:, bit], part(outs[place])))
            stores.append((view(theirs).at[:, 1 - bit], part(there)))

        def load():
            return [pltpu.make_async_copy(*one, in_sems.at[i]) for i, one in enumerate(loads)]

        def store():
            return [pltpu.make_async_copy(*one, out_sems.at[i]) for i, one in enumerate(stores)]

        def begin():
            for one in load():
                one.start()

        def work():
            for one in load():
                one.wait()
            for chain, mine, theirs in sums:
                if chain is None:
                    mine[:, bit] = mine[:, bit] + theirs[:, bit]
                    theirs[:, 1 - bit] = mine[:, 1 - bit] + theirs[:, 1 - bit]
                elif not isinstance(chain, Totals):
                    mine[...] = mine[...] + theirs[...]
                else:
                    half = chain.count // 2
                    high, low = chain.add(mine[...], theirs[...])
                    mine[0:half] = high
                    mine[half:] = low
            for one in store():
                one.start()

        def finish():
            for one in store():
                one.wait()

        return begin, work, finish


class Ride:
    def __init__(self, parts):
        self.parts = parts

    def begin(self):
        for begin, _, _ in self.parts:
            begin()

    def work(self):
        for _, work, _ in self.parts:
            work()

    def finish(self):
        for _, _, finish in self.parts:
            finish()


def kernel_call(
    kernel, name, marks, ins, in_specs, outs, out_specs, scratch, flops, after, steps, grid=(), weight=0.3, aliases=(), megabytes=MEGABYTES
):
    after = list(after)
    steps = [step for step in steps if step.chains]
    riders = [step for step in steps if step.fits]
    for step in steps:
        if not step.fits:
            keeps, send = step.plain()
            step.done(keeps, send)
            after.append(send)
    ride_ins = [step.operands() for step in riders]
    ride_outs = [step.outs() for step in riders]
    ride_scratch = [step.scratch() for step in riders]
    flat = lambda lists: [one for part in lists for one in part]

    def body(*refs):
        refs = list(refs)

        def take(count):
            taken = refs[:count]
            del refs[:count]
            return taken

        take(len(after))
        (marks_ref,) = take(1)
        r_ins = [take(len(part)) for part in ride_ins]
        used = take(len(ins) + len(outs))
        r_outs = [take(len(part)) for part in ride_outs]
        own = take(len(scratch))
        r_scratch = [take(len(part)) for part in ride_scratch]
        ride = Ride(
            [
                step.bind(marks_ref, *refs3)
                for step, *refs3 in zip(riders, r_ins, r_outs, r_scratch)
            ]
        )
        kernel(ride, marks_ref, *used, *own)

    results = pl.pallas_call(
        body,
        grid=grid,
        out_shape=[*outs, *flat(ride_outs)],
        in_specs=[ANY] * len(after) + [SMEM] + [ANY] * len(flat(ride_ins)) + in_specs,
        out_specs=[*out_specs] + [ANY] * len(flat(ride_outs)),
        scratch_shapes=[*scratch, *flat(ride_scratch)],
        compiler_params=pltpu.CompilerParams(vmem_limit_bytes=megabytes << 20),
        cost_estimate=pl.CostEstimate(
            flops=int(weight * flops), bytes_accessed=1 << 20, transcendentals=0
        ),
        input_output_aliases={
            len(after) + 1 + len(flat(ride_ins)) + one: other for one, other in aliases
        },
        name=name,
    )(*after, marks, *flat(ride_ins), *ins)
    made, rest = list(results[: len(outs)]), list(results[len(outs) :])
    for step, part in zip(riders, ride_outs):
        *keeps, send = rest[: len(part)]
        del rest[: len(part)]
        step.done(keeps, send)
    return made


class Place:
    def __init__(self, marks, extents, largest):
        self.height, self.breadth = extents[0, 0], extents[0, 1]
        self.own, self.core = marks[0], marks[1]
        self.big = largest[0] == self.own


def scaled(place, extent, level):
    product = (place * (extent >> level)).astype(F32) + 0.5
    return jnp.floor(product / extent.astype(F32)).astype(jnp.int32)


def sources(place, offset, count):
    spot = lax.broadcasted_iota(jnp.int32, (1, count), 1) + offset
    row, col = spot // CANVAS, spot % CANVAS
    valid = (row < place.height) & (col < place.breadth)
    half = scaled(row, place.height, 1) * CANVAS + scaled(col, place.breadth, 1)
    quarter = scaled(row, place.height, 2) * CANVAS + START_COL + scaled(col, place.breadth, 2)
    return jnp.where(valid, half, -1), jnp.where(valid, quarter, -1), jnp.where(valid, spot, -1)


def select_matrix(first, second, length):
    spot = lax.broadcasted_iota(jnp.int32, (length, first.shape[1]), 0)
    return ((spot == first).astype(F32) + (spot == second).astype(F32)).astype(BF16)


def pixel_mask(place):
    spot = lax.broadcasted_iota(jnp.int32, (PIXELS, 1), 0)
    row, col = spot // CANVAS, spot % CANVAS
    height, breadth = place.height, place.breadth
    large = ((row < height) & (col < breadth)).astype(F32)
    half = ((row < height >> 1) & (col < breadth >> 1)).astype(F32)
    quarter = (
        (row < height >> 2) & (col >= START_COL) & (col < START_COL + (breadth >> 2))
    ).astype(F32)
    return jnp.where(place.big, large, jnp.maximum(half, quarter))


def spread(values, pad, copies, base, dilation, flip, taps=(0, 1, 2)):
    if values is not None:
        pad[SIDE : SIDE + PIXELS] = values
    col = lax.broadcasted_iota(jnp.int32, (PIXELS, 1), 0) % CANVAS
    for tap in taps:
        shift = (1 - tap if flip else tap - 1) * dilation
        moved = pad[SIDE + shift : SIDE + shift + PIXELS]
        if shift != 0:
            inside = (col + shift >= 0) & (col + shift < CANVAS)
            moved = jnp.where(inside, moved, 0.0)
        copies[tap, base : base + PIXELS] = moved.astype(BF16)


def clear_edges(copies, base):
    width = copies.shape[2]
    for tap in range(3):
        copies[tap, base - EDGE : base] = jnp.zeros((EDGE, width), BF16)
        copies[tap, base + PIXELS : base + PIXELS + EDGE] = jnp.zeros((EDGE, width), BF16)


def tap_start(base, row_tap, dilation, flip):
    return base + (1 - row_tap if flip else row_tap - 1) * dilation * CANVAS


def forward_kernel(
    ride,
    marks,
    extents,
    largest,
    features,
    scale_hbm,
    shift_hbm,
    w1,
    w2,
    w3,
    w4,
    w5,
    w6,
    entered,
    top,
    g1,
    g2,
    g3,
    g4,
    g5,
    g6,
    weights,
    first,
    scale,
    shift,
    pad_in,
    pad,
    copies_in,
    copies,
    total,
    made_e,
    made_g,
    sems,
    out_sems,
    small_sems,
):
    kernels = (w1, w2, w3, w4, w5, w6)
    slopes = (g1, g2, g3, g4, g5, g6)
    copy = pltpu.make_async_copy

    def load(layer):
        rows = kernels[layer].shape[0]
        return copy(kernels[layer], weights.at[layer % 2, pl.ds(0, rows)], sems.at[layer % 2])

    def store_e(layer):
        there = top if layer == 6 else entered.at[pl.ds(layer * PIXELS, PIXELS)]
        return copy(made_e.at[layer % 2], there, out_sems.at[0, layer % 2])

    def store_g(layer):
        return copy(made_g.at[layer % 2], slopes[layer], out_sems.at[1, layer % 2])

    small = [
        copy(features, first, small_sems.at[0]),
        copy(scale_hbm, scale, small_sems.at[1]),
        copy(shift_hbm, shift, small_sems.at[2]),
    ]
    for one in small:
        one.start()
    load(0).start()
    mask = pixel_mask(Place(marks, extents, largest))
    clear_edges(copies_in, EDGE)
    clear_edges(copies, EDGE)
    for one in small:
        one.wait()
    fan = features.shape[1]
    current = first[...].astype(F32) * mask
    made_e[0] = jnp.zeros_like(made_e[0])
    made_e[0, :, 0:fan] = current.astype(BF16)
    store_e(0).start()
    for layer in range(6):
        dilation = DILATIONS[layer]
        fan = kernels[layer].shape[0] // 9
        source = copies_in if layer == 0 else copies
        spread(current, pad_in if layer == 0 else pad, source, EDGE, dilation, False)
        load(layer).wait()
        if layer + 1 < 6:
            load(layer + 1).start()
        for row_tap in range(3):
            begin = tap_start(EDGE, row_tap, dilation, False)
            for col_tap in range(3):
                tap = 3 * row_tap + col_tap
                part = jnp.dot(
                    source[col_tap, begin : begin + PIXELS],
                    weights[layer % 2, tap * fan : (tap + 1) * fan],
                    preferred_element_type=F32,
                )
                if tap == 0:
                    total[...] = part
                else:
                    total[...] += part
        factor = scale[layer : layer + 1]
        h = total[...] * factor + shift[layer : layer + 1]
        root = 0.7978845608028654
        square = h * h
        t = jnp.tanh(h * (root + 0.044715 * root * square))
        rise = 0.5 + 0.5 * t
        current = h * rise
        slope = rise + (current - current * t) * (root + 0.134145 * root * square)
        if layer >= 2:
            store_g(layer - 2).wait()
        if layer >= 1:
            store_e(layer - 1).wait()
        made_g[layer % 2] = (slope * (factor * mask)).astype(BF16)
        current = mask * current
        made_e[(layer + 1) % 2] = current.astype(BF16)
        store_e(layer + 1).start()
        store_g(layer).start()
    for layer in (4, 5):
        store_e(layer + 1).wait()
        store_g(layer).wait()


def run_forward(marks, facts, features, scale, shift, kernels, after):
    fan = features.shape[1]
    rows = kernels[1].shape[0]
    entered, top, *slopes = kernel_call(
        forward_kernel,
        "trunk_forward",
        marks,
        [*facts, features, scale, shift, *kernels],
        [SMEM] * 2 + [HBM] * 9,
        [shape(6 * PIXELS, C_MID)] + [shape(PIXELS, C_MID)] * 7,
        [HBM] * 8,
        [
            pltpu.VMEM((2, rows, C_MID), BF16),
            buffer(PIXELS, fan),
            buffer(6, C_MID, F32),
            buffer(6, C_MID, F32),
            buffer(PIXELS + 2 * SIDE, fan, F32),
            buffer(PIXELS + 2 * SIDE, C_MID, F32),
            pltpu.VMEM((3, PIXELS + 2 * EDGE, fan), BF16),
            pltpu.VMEM((3, PIXELS + 2 * EDGE, C_MID), BF16),
            buffer(PIXELS, C_MID, F32),
            pltpu.VMEM((2, PIXELS, C_MID), BF16),
            pltpu.VMEM((2, PIXELS, C_MID), BF16),
            pltpu.SemaphoreType.DMA((2,)),
            pltpu.SemaphoreType.DMA((2, 2)),
            pltpu.SemaphoreType.DMA((3,)),
        ],
        sum(2 * PIXELS * k.size for k in kernels),
        after,
        [],
        weight=2.5,
    )
    return entered, top, slopes


def head_chain(project, canvas_grad, factor):
    inverse = lax.rsqrt(jnp.sum(project * project, axis=1, keepdims=True) + 1e-06)
    made = (project * inverse * factor).astype(BF16)
    scaled_grad = canvas_grad * inverse
    product = scaled_grad * project
    gain_grad = jnp.sum(product, axis=0, keepdims=True)
    inner = jnp.sum(product * factor, axis=1, keepdims=True) * (inverse * inverse)
    return made, (scaled_grad * factor - project * inner).astype(BF16), gain_grad


def head_kernel(split, ride, marks, extents, largest, labels, grad_own, grad_other, *rest):
    taps, heads, gains = rest[0:2], rest[2:4], rest[4]
    out, send_out, _, *rest = rest[5:]
    if split:
        keeps, sends, rest = rest[0:2], rest[2:4], rest[4:]
    else:
        keeps, sends, rest = rest[0:2], None, rest[2:]
    gain_grads, tap_grads, rest = rest[0:2], rest[2:4], rest[4:]
    picks, grads, block, *turned = rest
    step = pl.program_id(0)
    place = Place(marks, extents, largest)
    own = place.own

    @pl.when(step == 0)
    def _():
        ride.begin()
        half, quarter, same = sources(place, 0, PIXELS)
        labelled = labels[...] == 1
        first = jnp.where(place.big, same, half)
        second = jnp.where(place.big, -1, quarter)
        picks[...] = select_matrix(
            jnp.where(labelled, first, -1), jnp.where(labelled, second, -1), PIXELS
        )
        for i in range(2):
            turned[i][...] = taps[i][...].T

    def some_heads(count):
        wide = slice(0, count * TASK_C)
        grads[pl.ds(aligned(own * HALF), HALF), wide] = grad_own[:, wide]
        grads[pl.ds(aligned((1 - own) * HALF), HALF), wide] = grad_other[:, wide]
        projects = [
            jnp.dot(taps[i][...], heads[i][:, wide], preferred_element_type=F32) for i in range(2)
        ]
        canvas_grad = jnp.dot(picks[...], grads[:, wide], preferred_element_type=F32)
        made = []
        for i in range(2):
            parts = []
            for head in range(count):
                columns = slice(head * TASK_C, (head + 1) * TASK_C)
                output, dproject, gain_grad = head_chain(
                    projects[i][:, columns], canvas_grad[:, columns], gains[i : i + 1, columns]
                )
                gain_grads[i][:, columns] = gain_grad
                parts.append((output, dproject))
            made.append(jnp.concatenate([part[0] for part in parts], axis=1))
            dproject = jnp.concatenate([part[1] for part in parts], axis=1)
            weight_grad = jnp.dot(
                turned[i][...], dproject, preferred_element_type=F32
            ).astype(BF16)
            if split:
                first = place.core == 0
                for head in range(count):
                    columns = slice(head * TASK_C, (head + 1) * TASK_C)
                    runs = weight_grad[:, columns].reshape(
                        C_MID // (2 * split), 2, split // 16, 16, TASK_C
                    )
                    ours = jnp.where(first, runs[:, 0], runs[:, 1])
                    others = jnp.where(first, runs[:, 1], runs[:, 0])
                    keeps[i][:, head] = ours.reshape(C_MID // 32, 16, TASK_C)
                    sends[i][:, head] = others.reshape(C_MID // 32, 16, TASK_C)
            else:
                keeps[i][:, wide] = weight_grad
            back = lax.dot_general(
                dproject,
                heads[i][:, wide],
                (((1,), (1,)), ((), ())),
                preferred_element_type=F32,
            )
            tap_grads[i][...] = jnp.where(step == 0, 0.0, tap_grads[i][...]) + back
        block[:, wide] = (made[0].astype(F32) + made[1].astype(F32)).astype(BF16)
        out[:, wide] = block[:, wide]
        start = jnp.where(place.big, (1 - own) * HALF, 0)
        send_out[:, wide] = block[pl.ds(aligned(start), HALF), wide]

    @pl.when(step < TASKS // 2)
    def _():
        some_heads(2)

    @pl.when(step == TASKS // 2)
    def _():
        some_heads(1)
        ride.work()
        ride.finish()


def run_heads(marks, facts, labels, grad_own, grad_other, tops, heads, gains, after, steps):
    pair = 2 * TASK_C
    tile = lambda rows: pl.BlockSpec((rows, pair), lambda i: (0, i))
    whole = lambda shape: pl.BlockSpec(shape, lambda i: (0, 0))
    chains = [Chain(1, TASKS * C_MID) for _ in range(2)]
    split = chains[0].run(0) // TASKS
    if chains[0].block == 16 * TASKS:
        blocks = C_MID // 32
        grads = [jax.ShapeDtypeStruct((blocks, TASKS, 16, TASK_C), BF16)] * 4
        grad_specs = [pl.BlockSpec((blocks, 2, 16, TASK_C), lambda i: (0, i, 0, 0))] * 4
    else:
        split = None
        grads = [shape(C_MID, HEAD_OUT)] * 2
        grad_specs = [tile(C_MID)] * 2
    out, send_out, entered, *made = kernel_call(
        functools.partial(head_kernel, split),
        "heads",
        marks,
        [
            *facts,
            labels,
            grad_own,
            grad_other,
            *tops,
            *heads,
            jnp.stack(gains),
        ],
        [SMEM] * 2
        + [whole((1, PIXELS))]
        + [tile(HALF)] * 2
        + [whole((PIXELS, C_MID)), pl.BlockSpec((PIXELS, C_MID), lambda i: (3, 0))]
        + [tile(C_MID)] * 2
        + [tile(2)],
        [shape(PIXELS, HEAD_OUT), shape(HALF, HEAD_OUT), shape(*tops[1].shape)]
        + grads
        + [shape(1, HEAD_OUT, F32)] * 2
        + [shape(PIXELS, C_MID, F32)] * 2,
        [tile(PIXELS), tile(HALF), HBM]
        + grad_specs
        + [tile(1)] * 2
        + [whole((PIXELS, C_MID))] * 2,
        [buffer(PIXELS, PIXELS), buffer(PIXELS, pair), buffer(PIXELS, pair)]
        + [buffer(C_MID, PIXELS)] * 2,
        4 * PIXELS * HEAD_OUT * (3 * C_MID + PIXELS),
        after,
        steps,
        grid=(TASKS // 2 + 1,),
        aliases=[(6, 2)],
    )
    if split is None:
        parts, made = made[:2], made[2:]
        for chain, part in zip(chains, parts):
            blocks = part.reshape(-1, chain.block // TASKS, TASKS, TASK_C).swapaxes(1, 2)
            first_exchange(chain, 0, blocks.reshape(-1, TASK_C), None)
    else:
        keeps, sends, made = made[:2], made[2:4], made[4:]
        for chain, keep, send in zip(chains, keeps, sends):
            first_exchange(chain, 0, keep.reshape(-1, TASK_C), send.reshape(-1, TASK_C))
    gain_grads = [part.reshape(TASKS, TASK_C) for part in made[:2]]
    return out, send_out, entered, chains, gain_grads, made[2:]


def first_exchange(chain, name, keep, send):
    if send is None:
        run = chain.run(name)
        bit = own_bit(name)
        width = chain.width
        whole = keep.reshape(-1, 2, run, width)
        choose = lambda which: lax.dynamic_index_in_dim(whole, which, 1, keepdims=False)
        keep, send = choose(bit).reshape(-1, width), choose(1 - bit).reshape(-1, width)
    chain.remove(name, (keep, 0), (exchange(send, name), 0))


def merge_kernel(ride, marks, extents, largest, own, other, out, picks):
    step = pl.program_id(0)
    place = Place(marks, extents, largest)
    start = pl.multiple_of(place.own * HALF, HALF)

    @pl.when(step == 0)
    def _():
        ride.begin()
        half, quarter, _ = sources(place, start, HALF)
        picks[...] = select_matrix(half, quarter, HALF)

    @pl.when(step == 3)
    def _():
        ride.work()

    def add(coarse, fine):
        read = lax.dot_general(
            picks[...], coarse, (((0,), (0,)), ((), ())), preferred_element_type=F32
        )
        out[...] = (read + fine.astype(F32)).astype(BF16)

    @pl.when(place.big)
    def _():
        add(other[...], own[pl.ds(start, HALF)])

    @pl.when(jnp.logical_not(place.big))
    def _():
        add(own[0:HALF], other[...])

    @pl.when(step == TASKS - 1)
    def _():
        ride.finish()


def run_merge(marks, facts, own, other, after, steps):
    tile = lambda rows: pl.BlockSpec((rows, TASK_C), lambda i: (0, i))
    (out,) = kernel_call(
        merge_kernel,
        "merge",
        marks,
        [*facts, own, other],
        [SMEM] * 2 + [tile(PIXELS), tile(HALF)],
        [shape(HALF, HEAD_OUT)],
        [tile(HALF)],
        [buffer(HALF, HALF)],
        2 * HALF * HALF * HEAD_OUT,
        after,
        steps,
        grid=(TASKS,),
        weight=20,
    )
    return out


class BackTask:
    def __init__(self, depth, weights, slope, grads):
        self.depth, self.ins = depth, [weights, slope, *grads]
        self.final = depth == 0
        self.rows = weights.shape[0]
        self.fan = self.rows // 9
        self.flops = 2 * PIXELS * weights.size

    def scratch(self):
        return [
            buffer(self.rows, C_MID),
            buffer(PIXELS, C_MID),
            buffer(PIXELS, C_MID, F32),
            buffer(PIXELS, C_MID, F32),
            pltpu.VMEM((2, PIXELS, WIDTH), BF16),
            buffer(PIXELS + 2 * SIDE, C_MID, F32),
            pltpu.VMEM((3, PIXELS + 2 * EDGE, C_MID), BF16),
            buffer(PIXELS, self.fan, F32),
            buffer(PIXELS, self.fan),
            pltpu.SemaphoreType.DMA((3,)),
            pltpu.SemaphoreType.DMA((3,)),
            pltpu.SemaphoreType.DMA((3,)),
        ]

    def bind(self, place, marks, ins, scratch, own, other, back, above):
        self.place, self.above, self.back = place, above, back
        weights_hbm, slope_hbm, *grads_hbm = ins
        weights, slope, grad, more, halves, pad, copies, total, made, sems, in_sems, out_sems = scratch
        self.weights, self.slope, self.grads = weights, slope, [grad, more][: len(grads_hbm)]
        self.pad, self.copies, self.total, self.halves = pad, copies, total, halves
        copy = pltpu.make_async_copy
        wide = lambda ref: ref.reshape(3, 3, self.fan, C_MID)
        self.loads = [
            copy(wide(weights_hbm).at[:, column], wide(weights).at[:, column], sems.at[column])
            for column in range(3)
        ]
        self.small = [copy(slope_hbm, slope, in_sems.at[0])]
        for i, (there, here) in enumerate(zip(grads_hbm, self.grads)):
            self.small.append(copy(there, here, in_sems.at[1 + i]))
        self.stores = [
            copy(halves.at[0], own, out_sems.at[0]),
            copy(halves.at[1], other, out_sems.at[1]),
        ]
        self.made = made
        if back is not None:
            self.stores.append(copy(made if self.final else total, back, out_sems.at[2]))

    def start(self):
        for one in self.small:
            one.start()
        self.loads[1].start()

    def start_rest(self):
        self.loads[0].start()
        self.loads[2].start()

    def prepare(self, head=False):
        clear_edges(self.copies, EDGE)
        for one in self.small:
            one.wait()
        if head:
            self.start_rest()
        else:
            for one in self.loads:
                one.wait()
        self.head = head
        parts = [self.above.total] if self.above is not None else []
        parts += self.grads
        grad = parts[0][...]
        for part in parts[1:]:
            grad = grad + part[...]
        grad = grad * self.slope[...].astype(F32)
        rounded = grad.astype(BF16)
        low, high = rounded[:, :WIDTH], rounded[:, WIDTH:]
        first = self.place.core == 0
        self.halves[0] = jnp.where(first, low, high)
        self.halves[1] = jnp.where(first, high, low)
        self.stores[0].start()
        self.stores[1].start()
        self.spread(grad, 1)

    def spread(self, values, tap):
        spread(values, self.pad, self.copies, EDGE, DILATIONS[self.depth], True, (tap,))

    def tap(self, turn):
        if turn in (1, 4):
            self.spread(None, 0 if turn == 1 else 2)
        column = (1, 0, 2)[turn // 3]
        tap = 3 * (turn % 3) + column
        begin = tap_start(EDGE, tap // 3, DILATIONS[self.depth], True)
        if turn % 3 == 0 and self.head:
            self.loads[column].wait()
        part = lax.dot_general(
            self.copies[tap % 3, begin : begin + PIXELS],
            self.weights[tap * self.fan : (tap + 1) * self.fan],
            (((1,), (1,)), ((), ())),
            preferred_element_type=F32,
        )
        if turn == 0:
            self.total[...] = part
        else:
            self.total[...] += part

    def end(self):
        if self.back is not None:
            if self.final:
                self.made[...] = (self.total[...] * pixel_mask(self.place)).astype(BF16)
            self.stores[2].start()

    def finish(self):
        for one in self.stores:
            one.wait()


class WeightTask:
    def __init__(self, depth, fan, firsts, mine, theirs, grad_mine, grad_theirs):
        self.depth, self.fan, self.firsts = depth, fan, firsts
        self.spots = [grad_mine[1], grad_theirs[1]]
        self.ins = [mine, theirs, grad_mine[0], grad_theirs[0]]
        self.rows = 9 * fan
        self.width = WIDTH // len(firsts)
        self.chains = [Chain(1, self.rows, self.width) for _ in firsts]
        splits = [chain.run(first) for chain, first in zip(self.chains, firsts)]
        self.splits = [None if split % 16 else split for split in splits]
        self.flops = 4 * PIXELS * self.rows * WIDTH

    def outs(self):
        made = []
        for split in self.splits:
            if split is None:
                made.append(shape(self.rows, self.width))
            else:
                made += [shape(self.rows // 2, self.width)] * 2
        return made

    def scratch(self):
        return (
            [
                pltpu.VMEM((2, PIXELS, WIDTH), BF16),
                buffer(PIXELS + 2 * SIDE, WIDTH, F32),
                buffer(PIXELS + 2 * SIDE, WIDTH, F32),
                pltpu.VMEM((3, 2 * PIXELS + 4 * EDGE, WIDTH), BF16),
                buffer(2 * PIXELS, self.fan),
                pltpu.SemaphoreType.DMA((4,)),
            ]
            + [buffer(self.rows, self.width)] * len(self.firsts)
            + [
                pltpu.SemaphoreType.DMA((1 if split is None else self.rows // split,))
                for split in self.splits
            ]
        )

    def bind(self, marks, ins, outs, scratch):
        mine, theirs, grad_mine, grad_theirs = ins
        grads, pad, pad_two, copies, both, in_sems, *rest = scratch
        self.grads, self.pads, self.copies, self.both = grads, (pad, pad_two), copies, both
        self.parts, out_sems = rest[: len(self.splits)], rest[len(self.splits) :]
        copy = pltpu.make_async_copy
        rows = pl.ds(self.depth * PIXELS, PIXELS)
        fan = pl.ds(0, self.fan)
        self.small = [
            copy(grad_mine.at[pl.ds(self.spots[0], PIXELS)], grads.at[0], in_sems.at[0]),
            copy(grad_theirs.at[pl.ds(self.spots[1], PIXELS)], grads.at[1], in_sems.at[1]),
        ]
        self.loads = [
            copy(mine.at[rows, fan], both.at[pl.ds(0, PIXELS)], in_sems.at[2]),
            copy(theirs.at[rows, fan], both.at[pl.ds(PIXELS, PIXELS)], in_sems.at[3]),
        ]
        self.stores = []
        outs = list(outs)
        for split, name, part, sems in zip(self.splits, self.firsts, self.parts, out_sems):
            if split is None:
                self.stores.append((copy(part, outs.pop(0), sems.at[0]), self.rows))
                continue
            bit = marks[mark(name)]
            keep, send = outs.pop(0), outs.pop(0)
            for run in range(self.rows // (2 * split)):
                there = pl.ds(run * split, split)
                for side, (array, which) in enumerate(((keep, bit), (send, 1 - bit))):
                    here = pl.ds(aligned((2 * run + which) * split), split)
                    one = copy(part.at[here], array.at[there], sems.at[2 * run + side])
                    self.stores.append((one, (2 * run + 2) * split))

    def start(self):
        for one in self.small:
            one.start()

    def start_rest(self):
        for one in self.loads:
            one.start()

    def prepare(self, head=False):
        if head:
            self.start_rest()
        second = 2 * EDGE + PIXELS + EDGE
        for place, base in enumerate((EDGE, second)):
            clear_edges(self.copies, base)
            self.small[place].wait()
            values = self.grads[place].astype(F32)
            spread(values, self.pads[place], self.copies, base, DILATIONS[self.depth], True)
        for one in self.loads:
            one.wait()

    def tap(self, tap):
        dilation = DILATIONS[self.depth]
        begin = tap_start(EDGE, tap // 3, dilation, True)
        later = tap_start(2 * EDGE + PIXELS + EDGE, tap // 3, dilation, True)
        copies = self.copies
        shifted = jnp.concatenate(
            [copies[tap % 3, begin : begin + PIXELS], copies[tap % 3, later : later + PIXELS]],
            axis=0,
        )
        product = lax.dot_general(
            self.both[...], shifted, (((0,), (0,)), ((), ())), preferred_element_type=F32
        ).astype(BF16)
        rows = slice(tap * self.fan, (tap + 1) * self.fan)
        for place, part in enumerate(self.parts):
            part[rows] = product[:, place * self.width : (place + 1) * self.width]
        for one, last in self.stores:
            if tap * self.fan < last <= (tap + 1) * self.fan:
                one.start()

    def end(self):
        pass

    def finish(self):
        for one, _ in self.stores:
            one.wait()

    def take(self, made):
        for chain, first, split in zip(self.chains, self.firsts, self.splits):
            keep = made.pop(0)
            first_exchange(chain, first, keep, None if split is None else made.pop(0))


def gradient_kernel(tasks, ride, marks, extents, largest, *rest):
    rest = list(rest)

    def take(count):
        taken = rest[:count]
        del rest[:count]
        return taken

    place = Place(marks, extents, largest)
    backs = [task for task in tasks if isinstance(task, BackTask)]
    middle = (len(tasks) - 1) // 2
    ins = [take(len(task.ins)) for task in tasks]
    own, other, back = take(3) if backs else (None, None, None)
    outs = [take(len(task.outs())) if isinstance(task, WeightTask) else None for task in tasks]
    above = None
    for task, task_ins, task_outs in zip(tasks, ins, outs):
        scratch = take(len(task.scratch()))
        if isinstance(task, WeightTask):
            task.bind(marks, task_ins, task_outs, scratch)
        else:
            rows = pl.ds(backs.index(task) * PIXELS, PIXELS)
            last = back if task is backs[-1] else None
            task.bind(place, marks, task_ins, scratch, own.at[rows], other.at[rows], last, above)
            above = task
    tasks[0].start()
    tasks[0].prepare(True)
    ride.begin()
    for number, task in enumerate(tasks):
        following = tasks[number + 1] if number + 1 < len(tasks) else None
        free = isinstance(following, WeightTask) or following is not None and following.above is None
        for tap in range(9):
            if tap == 1 and following is not None:
                following.start()
                following.start_rest()
            task.tap(tap)
            if tap == 4 and free:
                following.prepare()
            if tap == 5 and number == middle:
                ride.work()
        task.end()
        if following is not None and not free:
            following.prepare()
    for task in tasks:
        task.finish()
    ride.finish()


def run_gradients(marks, facts, tasks, after, steps):
    backs = [task for task in tasks if isinstance(task, BackTask)]
    weights = [task for task in tasks if isinstance(task, WeightTask)]
    outs = []
    if backs:
        rows = len(backs) * PIXELS
        last = backs[-1]
        outs += [shape(rows, WIDTH), shape(rows, WIDTH)]
        outs.append(shape(PIXELS, last.fan, BF16 if last.final else F32))
    for task in weights:
        outs += task.outs()
    made = kernel_call(
        functools.partial(gradient_kernel, tasks),
        "gradients",
        marks,
        [*facts, *[one for task in tasks for one in task.ins]],
        [SMEM] * 2 + [HBM] * sum(len(task.ins) for task in tasks),
        outs,
        [HBM] * len(outs),
        [one for task in tasks for one in task.scratch()],
        sum(task.flops for task in tasks),
        after,
        steps,
    )
    token = made[0]
    own = other = back = None
    if backs:
        own, other, back = made[:3]
        made = made[3:]
    for task in weights:
        task.take(made)
    return own, other, back, token


def joined(mine, other):
    core = own_bit(0)
    left, right = jnp.where(core == 0, mine, other), jnp.where(core == 0, other, mine)
    return jnp.concatenate([left, right], axis=1).reshape(-1)


def stacked(total):
    return total.reshape(TASKS, -1, TASK_C).swapaxes(0, 1).reshape(-1)


def final_kernel(layout, marks, *refs):
    count = len(layout)
    first = marks[1] == 0
    for (rows, whole, doubled, spot, other_spot), mine, other, out in zip(
        layout, refs[:count], refs[count : 2 * count], refs[2 * count :]
    ):
        mine = mine[spot : spot + rows].astype(F32)
        other = other[other_spot : other_spot + rows].astype(F32)
        if doubled:
            rows = rows // 2
            lower = marks[0] == 0
            mine = jnp.where(lower, mine[:rows], mine[rows:])
            other = jnp.where(lower, other[:rows], other[rows:])
        if whole:
            left, right = jnp.where(first, mine, other), jnp.where(first, other, mine)
            for part in range(4):
                half = left if part < 2 else right
                columns = slice(part % 2 * 128, part % 2 * 128 + 128)
                out[pl.ds(part, rows, stride=4)] = half[:, columns]
        else:
            total, block = mine + other, rows // TASKS
            for head in range(TASKS):
                for part in range(2):
                    out[pl.ds(2 * head + part, block, stride=2 * TASKS)] = total[
                        head * block : (head + 1) * block, part * 128 : part * 128 + 128
                    ]


def final_rows(marks, kernels, heads=()):
    chains = [*kernels, *heads]
    if any(chain.block % 8 for chain in chains):
        made = []
        for chain in chains:
            rows = chain.rows()
            mine = rows_of(chain.keep, rows).astype(F32)
            other = rows_of(chain.came, rows).astype(F32)
            made.append(joined(mine, other) if chain in kernels else stacked(mine + other))
        return made
    layout = [
        (chain.rows(), place < len(kernels), chain.doubled, chain.keep[1], chain.came[1])
        for place, chain in enumerate(chains)
    ]
    made = pl.pallas_call(
        functools.partial(final_kernel, layout),
        out_shape=[
            shape(rows * (4 if whole else 2) // (2 if doubled else 1), 128, F32)
            for rows, whole, doubled, _, _ in layout
        ],
        in_specs=[SMEM] + [VMEM] * (2 * len(chains)),
        out_specs=[VMEM] * len(chains),
        compiler_params=pltpu.CompilerParams(vmem_limit_bytes=24 << 20),
        name="final_rows",
    )(marks, *[chain.keep[0] for chain in chains], *[chain.came[0] for chain in chains])
    return [one.reshape(-1) for one in made]


def on_device(
    features,
    extents,
    canvas_large,
    label_mask,
    kernel_one,
    kernel_two,
    kernel_three,
    kernel_four,
    kernel_five,
    kernel_six,
    affine_scale,
    affine_shift,
    head_lower,
    head_upper,
    gain_lower,
    gain_upper,
    merged_grad,
):
    kernels = (kernel_one, kernel_two, kernel_three, kernel_four, kernel_five, kernel_six)
    own = lax.axis_index("scale")
    marks = jnp.stack([own] + [own_bit(i) for i in range(bits())]).astype(jnp.int32)
    facts = (extents, canvas_large)
    far = list(range(2, bits()))

    grad_own = merged_grad.reshape(HALF, HEAD_OUT)
    grad_other = exchange(grad_own, "scale")
    labels = label_mask.reshape(1, HALF)
    labels_other = exchange(labels, "scale")
    labels = jnp.where(
        own == 0,
        jnp.concatenate([labels, labels_other], axis=1),
        jnp.concatenate([labels_other, labels], axis=1),
    )

    entered, top, slopes = run_forward(
        marks,
        facts,
        features.reshape(PIXELS, -1),
        affine_scale,
        affine_shift,
        kernels,
        [],
    )
    halves = {}

    def backward(depth, *grads):
        return BackTask(depth, kernels[depth], slopes[depth], grads)

    def weight(depth, *firsts):
        fan = kernels[depth].shape[0] // 9
        return WeightTask(depth, fan, firsts, entered, partner, *halves.pop(depth))

    def gradients(after, steps, *tasks):
        own_halves, other, back, token = run_gradients(marks, facts, tasks, after, steps)
        depths = [task.depth for task in tasks if isinstance(task, BackTask)]
        if depths:
            came = exchange(other, 0)
            for place, depth in enumerate(depths):
                halves[depth] = ((own_halves, place * PIXELS), (came, place * PIXELS))
        return back, token

    z0 = 2 if far else 1
    summed_taps, taps_send, entered, (u, l), gain_grads, (back, back_lower) = run_heads(
        marks,
        facts,
        labels,
        grad_own,
        grad_other,
        (top, entered),
        (head_upper, head_lower),
        (gain_upper, gain_lower),
        [],
        [],
    )
    gain_grads = gain_grads[::-1]
    partner = exchange(entered, 0)
    taps_other = exchange(taps_send, "scale")
    gains = jnp.concatenate(gain_grads)
    gains = jnp.pad(gains, ((0, 16 - 2 * TASKS), (0, 0)))
    high = gains.astype(BF16)
    gains = Totals(jnp.concatenate([high, (gains - high.astype(F32)).astype(BF16)]))
    gains.remove(0, gains.keep, (exchange(gains.keep[0], 0), 0))
    def some(name, *chains):
        return Step(name, *[chain for chain in chains if name in chain.names])

    def batch(after, *steps):
        def kernel(ride, marks_ref):
            ride.begin()
            ride.work()
            ride.finish()

        steps = [step for step in steps if step.chains]
        if not steps:
            return after
        kernel_call(kernel, "sums", marks, [], [], [], [], [], 1, [after], steps)
        return steps[0].chains[0].keep[0]

    z1 = far[1] if far[1:] else None
    ul = (u, l)
    back, token = gradients([taps_send], [], backward(5, back), backward(4))
    t6, t5 = weight(5, 1), weight(4, z0)
    back, token = gradients([token], [], backward(3, back), backward(2, back_lower), t6, t5)
    (w6,), (w5,) = t6.chains, t5.chains
    t4, t3 = weight(3, 1), weight(2, z0)
    steps = [Step("scale", *ul)]
    back, token = gradients([token, taps_other], steps, backward(1, back), backward(0), t4, t3)
    (w4,), (w3,) = t4.chains, t3.chains
    t2, t1 = weight(1, "scale"), weight(0, 1)
    _, token = gradients([token], [some(z0, w6, gains), some(z1, w5)], t2, t1)
    (w2,), (w1,) = t2.chains, t1.chains
    merged = run_merge(marks, facts, summed_taps, taps_other, [token], [])
    order = batch(merged, some(z0, w4), Step("scale", w3), some(1, *ul))
    order = batch(order, some(1, w2), some(z1, w6), Step("scale", w5, gains), some(z0, w1))
    order = batch(order, some(z1, w4), some(1, w3), some(z0, *ul))
    order = batch(order, some(z0, w2), Step("scale", w6), some(1, w5, gains), some(z1, w1))
    order = batch(order, Step("scale", w4), some(z1, w3, gains), some(z1, *ul))
    for name in far[2:]:
        for chain in (u, l, w6, w5, w4, w3, w1):
            Step(name, chain).go()
    order = batch(order, some(z1, w2), Step(0, w6, w5), Step("scale", w1))
    for name in far[2:]:
        Step(name, w2).go()
        Step(name, gains).go()
    order = batch(order, Step(0, w4, w3))
    Step(0, w2, w1).go()
    g6, g5, gu, gl = final_rows(marks, [w6, w5], [u, l])
    g4, g3 = final_rows(marks, [w4, w3])
    g2, g1 = final_rows(marks, [w2, w1])

    share = HEAD_OUT // (lax.axis_size("img") * lax.axis_size("scale"))
    spot = lax.axis_index("img") * lax.axis_size("scale") + own
    added = gains.add(rows_of(gains.keep, gains.count), rows_of(gains.came, gains.count))
    added = added[0].astype(F32) + added[1].astype(F32)
    added = added[: 2 * TASKS].reshape(2, HEAD_OUT)
    gains = lax.dynamic_slice_in_dim(added, spot * share, share, 1)

    features_grad = back.reshape(features.shape)
    return (
        merged.reshape(merged_grad.shape),
        features_grad,
        *[g1, g2, g3, g4, g5, g6],
        gl,
        gu,
        gains[0],
        gains[1],
    )


def solution(mesh):
    in_specs = (
        P("img", "scale", None, None, None),
        P("img", None),
        P("img"),
        P("img", "scale", None),
        P(),
        P(),
        P(),
        P(),
        P(),
        P(),
        P(),
        P(),
        P(),
        P(),
        P(),
        P(),
        P("img", "scale", None, None),
    )
    out_specs = (
        P("img", "scale", None, None),
        P("img", "scale", None, None, None),
        P(("img", "scale")),
        P(("img", "scale")),
        P(("img", "scale")),
        P(("img", "scale")),
        P(("img", "scale")),
        P(("img", "scale")),
        P(("img", "scale")),
        P(("img", "scale")),
        P(("img", "scale")),
        P(("img", "scale")),
    )
    return jax.shard_map(
        on_device, mesh=mesh, in_specs=in_specs, out_specs=out_specs, check_vma=False
    )
```
